512 devices in a mesh: wide: 128 (over x, z, core), grp: 4 (over y).
Axes of the slice: x: 4, y: 4, z: 16, core: 2. Of those that a mesh axis runs over, the one named last changes fastest.
Arguments:
- query_rows: bfloat16 [65536, 1280], P(('wide', 'grp')), may hold values from -9 to 9, as said below
- key_rows: bfloat16 [65536, 1280], P(('wide', 'grp')), may hold values from -9 to 9, as said below
- value_rows: bfloat16 [65536, 1280], P(('wide', 'grp')), may hold values from -6 to 6
- block_image: int32 [512], replicated, may hold values from 0 to 126, never falling along the last dimension, each value on 1 to 8 neighbouring positions
Outputs:
- attended: bfloat16 [65536, 1280], P(('wide', 'grp'))
The draws below stay inside these ranges and needn't reach their ends.
Inputs may be any that keep to these rules, and one draw needn't show every extreme that they name: `query_rows`: Queries: entries bounded as stated. `key_rows`: Keys: entries bounded as stated. `block_image`: image numbers never fall along the window; every image covers 1 to 8 whole blocks and one covers exactly 8.
All inputs are finite; a program needn't handle non-finite values.
Results may differ from the reference program's by a relative error of at most 0.004.
Values may be sent and summed in bfloat16 or wider, within the bound.
No kernel may reach another device: no remote copies, remote signals or barrier semaphores. Data moves between devices by JAX's collectives and lax.ppermute only.
A program may use at most 64 MiB of HBM per device.

```python
import math
import jax
import jax.numpy as jnp
import numpy as np
from jax import lax

HEADS = 16
HDIM = 80
BLK = 128
MOST = 8
NBLK = 512
TOKENS = 65536
IMAGES = 127


def plant_pair(key):
    width = HEADS * HDIM
    queries = jnp.clip(1.5 * jax.random.normal(jax.random.fold_in(key, 7), (TOKENS, width)), -9.0, 9.0)
    key_table = jnp.clip(1.5 * jax.random.normal(jax.random.fold_in(key, 8), (TOKENS, width)), -9.0, 9.0)
    return (queries.astype(jnp.float32), key_table.astype(jnp.float32))


def draw_query_rows(key, part):
    return plant_pair(key)[0].astype(jnp.bfloat16)


def draw_key_rows(key, part):
    return plant_pair(key)[1].astype(jnp.bfloat16)


def level_of(own_key, dims, shards, smallest, largest):
    gain, own = 1.0, jax.random.fold_in(own_key, 6)
    for position, shards_of in shards:
        heights = jnp.exp(jax.random.uniform(jax.random.fold_in(own, position), (shards_of,), jnp.float32, smallest / len(shards), largest / len(shards)))
        gain = gain * jnp.repeat(heights, dims[position] // shards_of).reshape([-1 if axis == position else 1 for axis in range(len(dims))])
    return gain


def profile(count, total, limit, lean):
    weights = [(1 << 20) // math.isqrt(standing ** lean) + 1 for standing in range(2, count + 1)]
    rest, holding = total - limit - (count - 1), [1] * (count - 1)
    while rest > 0:
        candidates = [i for i in range(count - 1) if holding[i] < limit]
        whole, remaining = sum([weights[i] for i in candidates]), rest
        for i in candidates:
            addition = min(limit - holding[i], max(1, remaining * weights[i] // whole), rest)
            holding[i] = holding[i] + addition
            rest = rest - addition
    return np.array([limit] + holding)


def uneven(stream_key, amount, total, most, slope):
    if amount == 2:
        one = jax.random.randint(stream_key, (), max(1, total - most), min(most, total - 1) + 1)
        return jnp.stack([one, total - one])
    sizes = jnp.asarray(profile(amount, total, most, slope), jnp.int32)
    twos = (amount - 1) // 2
    giver, sink = sizes[1:1 + 2 * twos:2], sizes[2:2 + 2 * twos:2]
    room = jnp.minimum(giver - 1, most - sink)
    moved = jax.random.randint(jax.random.fold_in(stream_key, 1), (twos,), 0, 1 << 20) % (room + 1)
    sizes = sizes.at[1:1 + 2 * twos:2].set(giver - moved).at[2:2 + 2 * twos:2].set(sink + moved)
    return sizes[jax.random.permutation(jax.random.fold_in(stream_key, 2), amount)]


def bell_draw(own_key, extent, scale, limit, shards=(), held_as=jnp.bfloat16):
    gain = level_of(own_key, extent, shards, -0.22, 0.18) if shards else 1.0
    values = jax.random.normal(own_key, extent, jnp.float32) * scale * gain
    return jnp.minimum(jnp.maximum(values, -limit), limit).astype(held_as)


def setup_inputs(seed: int = 0) -> dict:
    arg_keys = jax.random.split(jax.random.key(seed), 5)
    query_rows = draw_query_rows(jax.random.fold_in(arg_keys[4], 71), 0)
    key_rows = draw_key_rows(jax.random.fold_in(arg_keys[4], 71), 0)
    value_rows = bell_draw(arg_keys[2], (TOKENS, HEADS * HDIM), 1.0, 6.0, ((0, 512),))
    block_image = jnp.searchsorted(jnp.cumsum(uneven(arg_keys[3], IMAGES, NBLK, MOST, 1)), jnp.arange(NBLK), side="right").astype(jnp.int32)
    return {"query_rows": query_rows, "key_rows": key_rows, "value_rows": value_rows, "block_image": block_image}


neg_large = -1e+30

def reference(query_rows, key_rows, value_rows, block_image):
    margin = (MOST - 1) * BLK
    span_rows = BLK + 2 * margin
    token_ids = jnp.broadcast_to(block_image[:, None], (NBLK, BLK)).reshape(-1).astype(jnp.int32)
    padded_ids = jnp.pad(token_ids, (margin, margin), constant_values=-1)
    padded_keys = jnp.pad(key_rows.reshape(TOKENS, HEADS, HDIM), ((margin, margin), (0, 0), (0, 0)))
    padded_values = jnp.pad(value_rows.reshape(TOKENS, HEADS, HDIM), ((margin, margin), (0, 0), (0, 0)))
    query_heads = query_rows.reshape(NBLK, BLK, HEADS, HDIM)
    scale_value = 1.0 / math.sqrt(HDIM)

    def one_block(block_index):
        first_row = (block_index * BLK).astype(jnp.int32)
        query_block = lax.dynamic_index_in_dim(query_heads, block_index, 0, keepdims=False).astype(jnp.float32)
        key_window = lax.dynamic_slice_in_dim(padded_keys, first_row, span_rows, 0).astype(jnp.float32)
        value_window = lax.dynamic_slice_in_dim(padded_values, first_row, span_rows, 0).astype(jnp.float32)
        id_window = lax.dynamic_slice_in_dim(padded_ids, first_row, span_rows, 0)
        query_ids = lax.dynamic_slice_in_dim(token_ids, first_row, BLK, 0)
        same_image = query_ids[:, None] == id_window[None, :]
        scores = jnp.einsum('qhd,khd->hqk', query_block, key_window) * scale_value
        scores = jnp.where(same_image[None], scores, neg_large)
        row_max = lax.optimization_barrier(jnp.max(scores, axis=-1, keepdims=True))
        weights = jnp.where(same_image[None], jnp.exp(scores - row_max), 0.0)
        denominator = lax.optimization_barrier(jnp.sum(weights, axis=-1))
        rounded = lax.optimization_barrier(weights.astype(jnp.bfloat16)).astype(jnp.float32)
        attended = jnp.einsum('hqk,khd->qhd', rounded, value_window) / jnp.transpose(denominator)[:, :, None]
        return attended.reshape(BLK, HEADS * HDIM).astype(jnp.bfloat16)
    blocks = lax.map(one_block, jnp.arange(NBLK, dtype=jnp.int32))
    return blocks.reshape(TOKENS, HEADS * HDIM)
```

```python
import math

import jax
import jax.numpy as jnp
from jax import lax
from jax.experimental import pallas as pl
from jax.experimental.pallas import tpu as pltpu
from jax.sharding import PartitionSpec as P

HDIM = 80
BLK = 128
PER = 8
HEADS_HERE = 2
WIDTH = HEADS_HERE * HDIM
SCALE_LOG2 = math.log2(math.e) / math.sqrt(HDIM)
FAR = 1e30
VMEM = pl.BlockSpec(memory_space=pltpu.VMEM)
SMEM = pl.BlockSpec(memory_space=pltpu.SMEM)
LIMIT = pltpu.CompilerParams(vmem_limit_bytes=24 * 1024 * 1024)
F32 = jnp.float32
BF16 = jnp.bfloat16


def split_kernel(*refs):
    out_ref = refs[-1]
    for place, ref in enumerate(refs[:-1]):
        turned = ref[...].T
        for part in range(PER):
            out_ref[part, place * WIDTH : (place + 1) * WIDTH, :] = turned[part * WIDTH : (part + 1) * WIDTH, :]


def split_heads(*arrays):
    return pl.pallas_call(
        split_kernel,
        out_shape=jax.ShapeDtypeStruct((PER, WIDTH * len(arrays), BLK), BF16),
        in_specs=[VMEM] * len(arrays),
        out_specs=VMEM,
        compiler_params=LIMIT,
        name="split_heads",
    )(*arrays)


def join_kernel(in_ref, out_ref):
    out_ref[...] = in_ref[...].reshape(PER * WIDTH, BLK).T


def join_heads(parts):
    return pl.pallas_call(
        join_kernel,
        out_shape=jax.ShapeDtypeStruct((BLK, PER * WIDTH), BF16),
        in_specs=[VMEM],
        out_specs=VMEM,
        compiler_params=LIMIT,
        name="join_heads",
    )(parts)


def both_heads(query):
    row = lax.broadcasted_iota(jnp.int32, (WIDTH, BLK), 0)
    none = jnp.zeros_like(query)
    return jnp.concatenate((jnp.where(row < HDIM, query, none), jnp.where(row < HDIM, none, query)), axis=1)


def diagonal(total):
    return jnp.concatenate((total[:HDIM, :BLK], total[HDIM:, BLK:]), axis=0)


def per_row(stat):
    return jnp.concatenate(
        (
            jnp.broadcast_to(stat[:, :BLK], (HDIM, BLK)),
            jnp.broadcast_to(stat[:, BLK:], (HDIM, BLK)),
        ),
        axis=0,
    )


def own_kernel(span_ref, kv_ref, q_ref, out_ref, acc_ref, max_ref, den_ref, keys, scores):
    for block in range(PER):
        keys[block * BLK : (block + 1) * BLK, :] = kv_ref[block, :WIDTH, :].T

    def one(i, carry):
        first, last = span_ref[0, i], span_ref[1, i]
        weights_in = both_heads(q_ref[i])
        top = jnp.full((1, 2 * BLK), -FAR, F32)
        for j in range(PER):
            rows = slice(j * BLK, (j + 1) * BLK)
            found = jnp.dot(keys[rows, :], weights_in, preferred_element_type=F32)
            scores[rows, :] = found
            inside = (j >= first) & (j < last)
            top = jnp.maximum(top, jnp.where(inside, jnp.max(found, axis=0, keepdims=True), -FAR))
        shift = top * SCALE_LOG2
        total = jnp.zeros((WIDTH, 2 * BLK), F32)
        den = jnp.zeros((1, 2 * BLK), F32)
        for j in range(PER):
            rows = slice(j * BLK, (j + 1) * BLK)
            inside = (j >= first) & (j < last)
            here = jnp.where(inside, shift, FAR)
            weights = jnp.exp2(scores[rows, :] * SCALE_LOG2 - here)
            den += jnp.sum(weights, axis=0, keepdims=True)
            total += jnp.dot(kv_ref[j, WIDTH:, :], weights.astype(BF16), preferred_element_type=F32)
        acc = diagonal(total)
        acc_ref[i] = acc
        max_ref[i] = top
        den_ref[i] = den
        out_ref[i] = (acc / per_row(den)).astype(BF16)
        return carry

    lax.fori_loop(0, PER, one, 0)


def own_part(span, kv, q):
    return pl.pallas_call(
        own_kernel,
        out_shape=(
            jax.ShapeDtypeStruct((PER, WIDTH, BLK), BF16),
            jax.ShapeDtypeStruct((PER, WIDTH, BLK), F32),
            jax.ShapeDtypeStruct((PER, 1, 2 * BLK), F32),
            jax.ShapeDtypeStruct((PER, 1, 2 * BLK), F32),
        ),
        in_specs=[SMEM, VMEM, VMEM],
        out_specs=(VMEM,) * 4,
        scratch_shapes=[pltpu.VMEM((PER * BLK, WIDTH), BF16), pltpu.VMEM((PER * BLK, 2 * BLK), F32)],
        compiler_params=LIMIT,
        cost_estimate=pl.CostEstimate(flops=4_000_000_000, bytes_accessed=4_000_000, transcendentals=2_000_000),
        name="own_part",
    )(span, kv, q)


def halo_kernel(span_ref, below_ref, above_ref, q_ref, start_ref, acc_ref, max_ref, den_ref, out_ref, keys):
    out_ref[...] = start_ref[...]

    def reach(kv_ref, row, first_query, last_query):
        low, high = span_ref[row, 0], span_ref[row, 1]

        def turn(j, carry):
            keys[pl.ds(pl.multiple_of(j * BLK, BLK), BLK), :] = kv_ref[j, :WIDTH, :].T
            return carry

        lax.fori_loop(low, high, turn, 0)

        def one(i, carry):
            weights_in = both_heads(q_ref[i])
            start = (acc_ref[i], max_ref[i], den_ref[i])

            def fold(j, state):
                acc, top, den = state
                found = jnp.dot(
                    keys[pl.ds(pl.multiple_of(j * BLK, BLK), BLK), :], weights_in, preferred_element_type=F32
                )
                new = jnp.maximum(top, jnp.max(found, axis=0, keepdims=True))
                fade = jnp.exp2((top - new) * SCALE_LOG2)
                weights = jnp.exp2(found * SCALE_LOG2 - new * SCALE_LOG2)
                den = den * fade + jnp.sum(weights, axis=0, keepdims=True)
                more = jnp.dot(kv_ref[j, WIDTH:, :], weights.astype(BF16), preferred_element_type=F32)
                return acc * per_row(fade) + diagonal(more), new, den

            acc, top, den = lax.fori_loop(low, high, fold, start)
            out_ref[i] = (acc / per_row(den)).astype(BF16)
            return carry

        lax.fori_loop(first_query, last_query, one, 0)

    reach(below_ref, 2, 0, span_ref[2, 2])
    reach(above_ref, 3, span_ref[3, 2], PER)


def halo_part(span, below, above, q, start, acc, top, den):
    return pl.pallas_call(
        halo_kernel,
        out_shape=jax.ShapeDtypeStruct((PER, WIDTH, BLK), BF16),
        in_specs=[SMEM] + [VMEM] * 7,
        out_specs=VMEM,
        scratch_shapes=[pltpu.VMEM((PER * BLK, WIDTH), BF16)],
        input_output_aliases={4: 0},
        compiler_params=LIMIT,
        cost_estimate=pl.CostEstimate(flops=1_000_000_000, bytes_accessed=4_000_000, transcendentals=1_000_000),
        name="halo_part",
    )(span, below, above, q, start, acc, top, den)


def shifted(value, steps):
    count = lax.axis_size("sup")
    pairs = [(i, i + steps) for i in range(count) if 0 <= i + steps < count]
    return lax.ppermute(value, "sup", pairs)


def spans(block_image):
    sup = lax.axis_index("sup")
    here = lax.dynamic_slice_in_dim(block_image, sup * PER, PER)
    low = jnp.sum((block_image[None, :] < here[:, None]).astype(jnp.int32), axis=1) - sup * PER
    high = jnp.sum((block_image[None, :] <= here[:, None]).astype(jnp.int32), axis=1) - sup * PER
    zeros = jnp.zeros((PER,), jnp.int32)
    below = zeros.at[0].set(PER + jnp.minimum(low[0], 0)).at[1].set(PER)
    below = below.at[2].set(jnp.where(low[0] < 0, jnp.sum((low < 0).astype(jnp.int32)), 0))
    above = zeros.at[1].set(jnp.maximum(high[PER - 1] - PER, 0))
    above = above.at[2].set(PER - jnp.sum((high > PER).astype(jnp.int32)))
    return jnp.stack((jnp.maximum(low, 0), jnp.minimum(high, PER), below, above))


def body(query_rows, key_rows, value_rows, block_image):
    group = ("core", "grp")
    span = spans(block_image)
    kv = lax.all_to_all(split_heads(key_rows, value_rows), group, 0, 0, tiled=True)
    q = split_heads(query_rows)
    kv, q = lax.optimization_barrier((kv, q))
    below = shifted(kv, 1)
    above = shifted(kv, -1)
    q = lax.all_to_all(q, group, 0, 0, tiled=True)
    start, acc, top, den = own_part(span, kv, q)
    result = halo_part(span, below, above, q, start, acc, top, den)
    back = lax.all_to_all(result, group, 0, 0, tiled=True)
    return join_heads(back)


def solution(mesh):
    per_group = mesh.shape["grp"]
    cores = PER // per_group
    devices = mesh.devices.reshape(-1, cores, per_group)
    inner = jax.sharding.Mesh(devices, ("sup", "core", "grp"))
    rows = P(("sup", "core", "grp"), None)
    return jax.shard_map(
        body,
        mesh=inner,
        in_specs=(rows, rows, rows, P()),
        out_specs=rows,
        check_vma=False,
    )
```

```python
import functools
import math

import jax
import jax.numpy as jnp
from jax import lax
from jax.experimental import pallas as pl
from jax.experimental.pallas import tpu as pltpu
from jax.sharding import PartitionSpec as P

HDIM = 80
BLK = 128
PER = 8
HEADS_HERE = 2
WIDTH = HEADS_HERE * HDIM
TILES = PER * WIDTH // BLK
SCALE_LOG2 = math.log2(math.e) / math.sqrt(HDIM)
FAR = 1e30
SLOTS = 16
STEP = 4
VMEM = pl.BlockSpec(memory_space=pltpu.VMEM)
SMEM = pl.BlockSpec(memory_space=pltpu.SMEM)
HBM = pl.BlockSpec(memory_space=pltpu.HBM)
LIMIT = pltpu.CompilerParams(vmem_limit_bytes=24 * 1024 * 1024)
F32 = jnp.float32
BF16 = jnp.bfloat16


def cost(flops):
    return pl.CostEstimate(flops=flops, bytes_accessed=1_000_000, transcendentals=0)


def split_kernel(*refs):
    count = len(refs) - 3
    sources, out_ref, held, sems = refs[:count], refs[count], refs[count + 1], refs[count + 2]
    copies = [pltpu.make_async_copy(ref, held.at[place], sems.at[place]) for place, ref in enumerate(sources)]
    for copy in copies:
        copy.start()
    for place, copy in enumerate(copies):
        copy.wait()
        for tile in range(TILES):
            turned = held[place, :, tile * BLK : (tile + 1) * BLK].T
            first = tile * BLK
            while first < (tile + 1) * BLK:
                part, row = divmod(first, WIDTH)
                size = min((tile + 1) * BLK - first, WIDTH - row)
                skip = first - tile * BLK
                out_ref[part, place * WIDTH + row : place * WIDTH + row + size, :] = turned[skip : skip + size, :]
                first += size


def split_heads(*arrays):
    count = len(arrays)
    return pl.pallas_call(
        split_kernel,
        out_shape=jax.ShapeDtypeStruct((PER, WIDTH * count, BLK), BF16),
        in_specs=[HBM] * count,
        out_specs=VMEM,
        scratch_shapes=[pltpu.VMEM((count, BLK, PER * WIDTH), BF16), pltpu.SemaphoreType.DMA((count,))],
        cost_estimate=cost(500_000_000 * count),
        name="split_heads",
    )(*arrays)


def join_kernel(in_ref, out_ref):
    out_ref[...] = in_ref[...].reshape(PER * WIDTH, BLK).T


def join_heads(parts):
    return pl.pallas_call(
        join_kernel,
        out_shape=jax.ShapeDtypeStruct((BLK, PER * WIDTH), BF16),
        in_specs=[VMEM],
        out_specs=VMEM,
        compiler_params=LIMIT,
        name="join_heads",
    )(parts)


def both_heads(query):
    row = lax.broadcasted_iota(jnp.int32, (WIDTH, BLK), 0)
    none = jnp.zeros_like(query)
    return jnp.concatenate((jnp.where(row < HDIM, query, none), jnp.where(row < HDIM, none, query)), axis=1)


def diagonal(total):
    return jnp.concatenate((total[:HDIM, :BLK], total[HDIM:, BLK:]), axis=0)


def per_row(stat):
    return jnp.concatenate(
        (
            jnp.broadcast_to(stat[:, :BLK], (HDIM, BLK)),
            jnp.broadcast_to(stat[:, BLK:], (HDIM, BLK)),
        ),
        axis=0,
    )


def own_kernel(span_ref, qkv_ref, out_ref, acc_ref, max_ref, den_ref, keys, scores):
    for block in range(PER):
        keys[block * BLK : (block + 1) * BLK, :] = qkv_ref[block, WIDTH : 2 * WIDTH, :].T

    def one(i, carry):
        first, last = span_ref[0, i], span_ref[1, i]
        weights_in = both_heads(qkv_ref[i, :WIDTH, :])
        top = jnp.full((1, 2 * BLK), -FAR, F32)
        for j in range(PER):
            rows = slice(j * BLK, (j + 1) * BLK)
            found = jnp.dot(keys[rows, :], weights_in, preferred_element_type=F32)
            scores[rows, :] = found
            inside = (j >= first) & (j < last)
            top = jnp.maximum(top, jnp.where(inside, jnp.max(found, axis=0, keepdims=True), -FAR))
        shift = top * SCALE_LOG2
        total = jnp.zeros((WIDTH, 2 * BLK), F32)
        den = jnp.zeros((1, 2 * BLK), F32)
        for j in range(PER):
            rows = slice(j * BLK, (j + 1) * BLK)
            inside = (j >= first) & (j < last)
            here = jnp.where(inside, shift, FAR)
            weights = jnp.exp2(scores[rows, :] * SCALE_LOG2 - here)
            den += jnp.sum(weights, axis=0, keepdims=True)
            total += jnp.dot(qkv_ref[j, 2 * WIDTH :, :], weights.astype(BF16), preferred_element_type=F32)
        acc = diagonal(total)
        acc_ref[i] = acc
        max_ref[i] = top
        den_ref[i] = den
        out_ref[i] = (acc * per_row(1.0 / den)).astype(BF16)
        return carry

    lax.fori_loop(0, PER, one, 0)


def own_part(span, qkv):
    return pl.pallas_call(
        own_kernel,
        out_shape=(
            jax.ShapeDtypeStruct((PER, WIDTH, BLK), BF16),
            jax.ShapeDtypeStruct((PER, WIDTH, BLK), F32),
            jax.ShapeDtypeStruct((PER, 1, 2 * BLK), F32),
            jax.ShapeDtypeStruct((PER, 1, 2 * BLK), F32),
        ),
        in_specs=[SMEM, VMEM],
        out_specs=(VMEM,) * 4,
        scratch_shapes=[pltpu.VMEM((PER * BLK, WIDTH), BF16), pltpu.VMEM((PER * BLK, 2 * BLK), F32)],
        compiler_params=LIMIT,
        cost_estimate=cost(100_000_000_000),
        name="own_part",
    )(span, qkv)


def fold_rows(values, how):
    return how(values.reshape(BLK // 8, 8, 2 * BLK), axis=0)


def halo_kernel(side, pair_ref, kv_ref, q_ref, start_ref, acc_ref, max_ref, den_ref, out_ref, *scratch):
    keys, scores, tops, shifts, sums, dens = scratch
    pairs = pair_ref[side, 2 * SLOTS]
    steps = (pairs + STEP - 1) // STEP
    out_ref[...] = start_ref[...]

    @pl.when(pairs > 0)
    def _():
        for block in range(PER - 1):
            keys[block] = kv_ref[block, :WIDTH, :].T
        for block in range(PER):
            tops[block] = jnp.broadcast_to(max_ref[block], (8, 2 * BLK))

        def look(step, carry):
            for lane in range(STEP):
                pair = step * STEP + lane
                i, j = pair_ref[side, pair], pair_ref[side, SLOTS + pair]
                found = jnp.dot(keys[j], both_heads(q_ref[i, :WIDTH, :]), preferred_element_type=F32)
                scores[pair] = found
                tops[i] = jnp.maximum(tops[i], fold_rows(found, jnp.max))
            return carry

        lax.fori_loop(0, steps, look, 0)
        for block in range(PER):
            shifts[block] = jnp.max(tops[block], axis=0, keepdims=True) * SCALE_LOG2
        sums[...] = jnp.zeros_like(sums)
        dens[...] = jnp.zeros_like(dens)

        def weigh(step, carry):
            for lane in range(STEP):
                pair = step * STEP + lane
                i, j = pair_ref[side, pair], pair_ref[side, SLOTS + pair]
                shift = jnp.where(pair < pairs, shifts[i], FAR)
                weights = jnp.exp2(scores[pair] * SCALE_LOG2 - shift)
                dens[i] += fold_rows(weights, jnp.sum)
                sums[i] += diagonal(jnp.dot(kv_ref[j, WIDTH:, :], weights.astype(BF16), preferred_element_type=F32))
            return carry

        lax.fori_loop(0, steps, weigh, 0)

        def close(i, carry):
            fade = jnp.exp2(max_ref[i] * SCALE_LOG2 - shifts[i])
            share = 1.0 / (den_ref[i] * fade + jnp.sum(dens[i], axis=0, keepdims=True))
            out_ref[i] = (acc_ref[i] * per_row(fade * share) + sums[i] * per_row(share)).astype(BF16)
            return carry

        lax.fori_loop(pair_ref[side, 0], pair_ref[side, pairs - 1] + 1, close, 0)


def halo_part(side, pairs, kv, q, start, acc, top, den):
    return pl.pallas_call(
        functools.partial(halo_kernel, side),
        out_shape=jax.ShapeDtypeStruct((PER, WIDTH, BLK), BF16),
        in_specs=[SMEM] + [VMEM] * 6,
        out_specs=VMEM,
        scratch_shapes=[
            pltpu.VMEM((PER - 1, BLK, WIDTH), BF16),
            pltpu.VMEM((SLOTS, BLK, 2 * BLK), F32),
            pltpu.VMEM((PER, 8, 2 * BLK), F32),
            pltpu.VMEM((PER, 1, 2 * BLK), F32),
            pltpu.VMEM((PER, WIDTH, BLK), F32),
            pltpu.VMEM((PER, 8, 2 * BLK), F32),
        ],
        compiler_params=LIMIT,
        cost_estimate=cost(1_000_000_000),
        name="halo_part",
    )(pairs, kv, q, start, acc, top, den)


def shifted(value, steps):
    count = lax.axis_size("sup")
    pairs = [(i, i + steps) for i in range(count) if 0 <= i + steps < count]
    return lax.ppermute(value, "sup", pairs)


def spans(block_image):
    sup = lax.axis_index("sup")
    here = lax.dynamic_slice_in_dim(block_image, sup * PER, PER)
    low = jnp.sum((block_image[None, :] < here[:, None]).astype(jnp.int32), axis=1) - sup * PER
    high = jnp.sum((block_image[None, :] <= here[:, None]).astype(jnp.int32), axis=1) - sup * PER
    span = jnp.stack((jnp.maximum(low, 0), jnp.minimum(high, PER)))
    keys = jnp.stack((jnp.maximum(-jnp.min(low), 0), jnp.maximum(jnp.max(high) - PER, 0)))[:, None]
    queries = jnp.stack((jnp.sum((low < 0).astype(jnp.int32)), jnp.sum((high > PER).astype(jnp.int32))))[:, None]
    side = jnp.arange(2)[:, None]
    order = jnp.arange(SLOTS)[None, :]
    count = jnp.maximum(keys, 1)
    query = jnp.clip(jnp.where(side == 0, 0, PER - queries) + order // count, 0, PER - 1)
    key = jnp.where(side == 0, PER - 1 - count, 0) + order % count
    return span, jnp.concatenate((query, key, jnp.broadcast_to(keys * queries, (2, SLOTS))), axis=1)


def regrouped(parts):
    return lax.all_to_all(parts, ("core", "grp"), 0, 0, tiled=True)


def body(query_rows, key_rows, value_rows, block_image):
    span, pairs = spans(block_image)
    qkv = regrouped(split_heads(query_rows, key_rows, value_rows))
    rising = qkv[1:, WIDTH:]
    below = shifted(rising, 1)
    qkv, rising = lax.optimization_barrier((qkv, rising))
    above = shifted(qkv[:-1, WIDTH:], -1)
    start, acc, top, den = own_part(span, qkv)
    result = halo_part(1, pairs, above, qkv, start, acc, top, den)
    result = halo_part(0, pairs, below, qkv, result, acc, top, den)
    return join_heads(regrouped(result))


def solution(mesh):
    per_group = mesh.shape["grp"]
    cores = PER // per_group
    devices = mesh.devices.reshape(-1, cores, per_group)
    inner = jax.sharding.Mesh(devices, ("sup", "core", "grp"))
    rows = P(("sup", "core", "grp"), None)
    return jax.shard_map(
        body,
        mesh=inner,
        in_specs=(rows, rows, rows, P()),
        out_specs=rows,
        check_vma=False,
    )
```

```python
import functools
import math

import jax
import jax.numpy as jnp
from jax import lax
from jax.experimental import pallas as pl
from jax.experimental.pallas import tpu as pltpu
from jax.sharding import PartitionSpec as P

HDIM = 80
BLK = 128
PER = 8
HEADS_HERE = 2
WIDTH = HEADS_HERE * HDIM
TILES = PER * WIDTH // BLK
SCALE_LOG2 = math.log2(math.e) / math.sqrt(HDIM)
FAR = 1e30
SLOTS = 16
STEP = 4
VMEM = pl.BlockSpec(memory_space=pltpu.VMEM)
SMEM = pl.BlockSpec(memory_space=pltpu.SMEM)
HBM = pl.BlockSpec(memory_space=pltpu.HBM)
LIMIT = pltpu.CompilerParams(vmem_limit_bytes=24 * 1024 * 1024)
F32 = jnp.float32
BF16 = jnp.bfloat16


def cost(flops):
    return pl.CostEstimate(flops=flops, bytes_accessed=1_000_000, transcendentals=0)


def split_kernel(*refs):
    count = len(refs) - 3
    sources, out_ref, held, sems = refs[:count], refs[count], refs[count + 1], refs[count + 2]
    copies = [pltpu.make_async_copy(ref, held.at[place], sems.at[place]) for place, ref in enumerate(sources)]
    for copy in copies:
        copy.start()
    for place, copy in enumerate(copies):
        copy.wait()
        for tile in range(TILES):
            turned = held[place, :, tile * BLK : (tile + 1) * BLK].T
            first = tile * BLK
            while first < (tile + 1) * BLK:
                part, row = divmod(first, WIDTH)
                size = min((tile + 1) * BLK - first, WIDTH - row)
                skip = first - tile * BLK
                out_ref[part, place * WIDTH + row : place * WIDTH + row + size, :] = turned[skip : skip + size, :]
                first += size


def split_heads(*arrays):
    count = len(arrays)
    return pl.pallas_call(
        split_kernel,
        out_shape=jax.ShapeDtypeStruct((PER, WIDTH * count, BLK), BF16),
        in_specs=[HBM] * count,
        out_specs=VMEM,
        scratch_shapes=[pltpu.VMEM((count, BLK, PER * WIDTH), BF16), pltpu.SemaphoreType.DMA((count,))],
        cost_estimate=cost(500_000_000 * count),
        name="split_heads",
    )(*arrays)


def join_kernel(in_ref, out_ref):
    out_ref[...] = in_ref[...].reshape(PER * WIDTH, BLK).T


def join_heads(parts):
    return pl.pallas_call(
        join_kernel,
        out_shape=jax.ShapeDtypeStruct((BLK, PER * WIDTH), BF16),
        in_specs=[VMEM],
        out_specs=VMEM,
        compiler_params=LIMIT,
        name="join_heads",
    )(parts)


def both_heads(query):
    row = lax.broadcasted_iota(jnp.int32, (WIDTH, BLK), 0)
    none = jnp.zeros_like(query)
    return jnp.concatenate((jnp.where(row < HDIM, query, none), jnp.where(row < HDIM, none, query)), axis=1)


def diagonal(total):
    return jnp.concatenate((total[:HDIM, :BLK], total[HDIM:, BLK:]), axis=0)


def per_row(stat):
    return jnp.concatenate(
        (
            jnp.broadcast_to(stat[:, :BLK], (HDIM, BLK)),
            jnp.broadcast_to(stat[:, BLK:], (HDIM, BLK)),
        ),
        axis=0,
    )


def own_kernel(span_ref, qkv_ref, out_ref, acc_ref, max_ref, den_ref, keys, scores):
    for block in range(PER):
        keys[block * BLK : (block + 1) * BLK, :] = qkv_ref[block, WIDTH : 2 * WIDTH, :].T

    def one(i, carry):
        first, last = span_ref[0, i], span_ref[1, i]
        weights_in = both_heads(qkv_ref[i, :WIDTH, :])
        top = jnp.full((1, 2 * BLK), -FAR, F32)
        for j in range(PER):
            rows = slice(j * BLK, (j + 1) * BLK)
            found = jnp.dot(keys[rows, :], weights_in, preferred_element_type=F32)
            scores[rows, :] = found
            inside = (j >= first) & (j < last)
            top = jnp.maximum(top, jnp.where(inside, jnp.max(found, axis=0, keepdims=True), -FAR))
        shift = top * SCALE_LOG2
        total = jnp.zeros((WIDTH, 2 * BLK), F32)
        den = jnp.zeros((1, 2 * BLK), F32)
        for j in range(PER):
            rows = slice(j * BLK, (j + 1) * BLK)
            inside = (j >= first) & (j < last)
            here = jnp.where(inside, shift, FAR)
            weights = jnp.exp2(scores[rows, :] * SCALE_LOG2 - here)
            den += jnp.sum(weights, axis=0, keepdims=True)
            total += jnp.dot(qkv_ref[j, 2 * WIDTH :, :], weights.astype(BF16), preferred_element_type=F32)
        acc = diagonal(total)
        acc_ref[i] = acc
        max_ref[i] = top
        den_ref[i] = den
        out_ref[i] = (acc * per_row(1.0 / den)).astype(BF16)
        return carry

    lax.fori_loop(0, PER, one, 0)


def own_part(span, qkv):
    return pl.pallas_call(
        own_kernel,
        out_shape=(
            jax.ShapeDtypeStruct((PER, WIDTH, BLK), BF16),
            jax.ShapeDtypeStruct((PER, WIDTH, BLK), F32),
            jax.ShapeDtypeStruct((PER, 1, 2 * BLK), F32),
            jax.ShapeDtypeStruct((PER, 1, 2 * BLK), F32),
        ),
        in_specs=[SMEM, VMEM],
        out_specs=(VMEM,) * 4,
        scratch_shapes=[pltpu.VMEM((PER * BLK, WIDTH), BF16), pltpu.VMEM((PER * BLK, 2 * BLK), F32)],
        compiler_params=LIMIT,
        cost_estimate=cost(100_000_000_000),
        name="own_part",
    )(span, qkv)


def fold_rows(values, how):
    return how(values.reshape(BLK // 8, 8, 2 * BLK), axis=0)


def halo_kernel(side, pair_ref, kv_ref, q_ref, start_ref, acc_ref, max_ref, den_ref, out_ref, *scratch):
    keys, scores, tops, shifts, sums, dens = scratch
    pairs = pair_ref[side, 2 * SLOTS]
    steps = (pairs + STEP - 1) // STEP
    out_ref[...] = start_ref[...]

    @pl.when(pairs > 0)
    def _():
        for block in range(PER - 1):
            keys[block] = kv_ref[block, :WIDTH, :].T
        for block in range(PER):
            tops[block] = jnp.broadcast_to(max_ref[block], (8, 2 * BLK))

        def look(step, carry):
            for lane in range(STEP):
                pair = step * STEP + lane
                i, j = pair_ref[side, pair], pair_ref[side, SLOTS + pair]
                found = jnp.dot(keys[j], both_heads(q_ref[i, :WIDTH, :]), preferred_element_type=F32)
                scores[pair] = found
                tops[i] = jnp.maximum(tops[i], fold_rows(found, jnp.max))
            return carry

        lax.fori_loop(0, steps, look, 0)
        for block in range(PER):
            shifts[block] = jnp.max(tops[block], axis=0, keepdims=True) * SCALE_LOG2
        sums[...] = jnp.zeros_like(sums)
        dens[...] = jnp.zeros_like(dens)

        def weigh(step, carry):
            for lane in range(STEP):
                pair = step * STEP + lane
                i, j = pair_ref[side, pair], pair_ref[side, SLOTS + pair]
                shift = jnp.where(pair < pairs, shifts[i], FAR)
                weights = jnp.exp2(scores[pair] * SCALE_LOG2 - shift)
                dens[i] += fold_rows(weights, jnp.sum)
                sums[i] += diagonal(jnp.dot(kv_ref[j, WIDTH:, :], weights.astype(BF16), preferred_element_type=F32))
            return carry

        lax.fori_loop(0, steps, weigh, 0)

        def close(i, carry):
            fade = jnp.exp2(max_ref[i] * SCALE_LOG2 - shifts[i])
            share = 1.0 / (den_ref[i] * fade + jnp.sum(dens[i], axis=0, keepdims=True))
            out_ref[i] = (acc_ref[i] * per_row(fade * share) + sums[i] * per_row(share)).astype(BF16)
            return carry

        lax.fori_loop(pair_ref[side, 0], pair_ref[side, pairs - 1] + 1, close, 0)


def halo_part(side, pairs, kv, q, start, acc, top, den):
    return pl.pallas_call(
        functools.partial(halo_kernel, side),
        out_shape=jax.ShapeDtypeStruct((PER, WIDTH, BLK), BF16),
        in_specs=[SMEM] + [VMEM] * 6,
        out_specs=VMEM,
        scratch_shapes=[
            pltpu.VMEM((PER - 1, BLK, WIDTH), BF16),
            pltpu.VMEM((SLOTS, BLK, 2 * BLK), F32),
            pltpu.VMEM((PER, 8, 2 * BLK), F32),
            pltpu.VMEM((PER, 1, 2 * BLK), F32),
            pltpu.VMEM((PER, WIDTH, BLK), F32),
            pltpu.VMEM((PER, 8, 2 * BLK), F32),
        ],
        compiler_params=LIMIT,
        cost_estimate=cost(1_000_000_000),
        name="halo_part",
    )(pairs, kv, q, start, acc, top, den)


def shifted(value, steps):
    count = lax.axis_size("sup")
    pairs = [(i, i + steps) for i in range(count) if 0 <= i + steps < count]
    return lax.ppermute(value, "sup", pairs)


def spans(block_image):
    sup = lax.axis_index("sup")
    here = lax.dynamic_slice_in_dim(block_image, sup * PER, PER)
    low = jnp.sum((block_image[None, :] < here[:, None]).astype(jnp.int32), axis=1) - sup * PER
    high = jnp.sum((block_image[None, :] <= here[:, None]).astype(jnp.int32), axis=1) - sup * PER
    span = jnp.stack((jnp.maximum(low, 0), jnp.minimum(high, PER)))
    keys = jnp.stack((jnp.maximum(-jnp.min(low), 0), jnp.maximum(jnp.max(high) - PER, 0)))[:, None]
    queries = jnp.stack((jnp.sum((low < 0).astype(jnp.int32)), jnp.sum((high > PER).astype(jnp.int32))))[:, None]
    side = jnp.arange(2)[:, None]
    order = jnp.arange(SLOTS)[None, :]
    count = jnp.maximum(keys, 1)
    query = jnp.clip(jnp.where(side == 0, 0, PER - queries) + order // count, 0, PER - 1)
    key = jnp.where(side == 0, PER - 1 - count, 0) + order % count
    return span, jnp.concatenate((query, key, jnp.broadcast_to(keys * queries, (2, SLOTS))), axis=1)


def regrouped(parts):
    return lax.all_to_all(parts, ("core", "grp"), 0, 0, tiled=True)


def body(query_rows, key_rows, value_rows, block_image):
    span, pairs = spans(block_image)
    qkv = regrouped(split_heads(query_rows, key_rows, value_rows))
    rising = qkv[1:, WIDTH:]
    below = shifted(rising, 1)
    qkv, rising = lax.optimization_barrier((qkv, rising))
    above = shifted(qkv[:-1, WIDTH:], -1)
    start, acc, top, den = own_part(span, qkv)
    result = halo_part(0, pairs, below, qkv, start, acc, top, den)
    result = halo_part(1, pairs, above, qkv, result, acc, top, den)
    return join_heads(regrouped(result))


def solution(mesh):
    per_group = mesh.shape["grp"]
    cores = PER // per_group
    devices = mesh.devices.reshape(-1, cores, per_group)
    inner = jax.sharding.Mesh(devices, ("sup", "core", "grp"))
    rows = P(("sup", "core", "grp"), None)
    return jax.shard_map(
        body,
        mesh=inner,
        in_specs=(rows, rows, rows, P()),
        out_specs=rows,
        check_vma=False,
    )
```

```python
import functools
import math

import jax
import jax.numpy as jnp
from jax import lax
from jax.experimental import pallas as pl
from jax.experimental.pallas import tpu as pltpu
from jax.sharding import PartitionSpec as P

HDIM = 80
BLK = 128
PER = 8
HEADS_HERE = 2
WIDTH = HEADS_HERE * HDIM
TILES = PER * WIDTH // BLK
SCALE_LOG2 = math.log2(math.e) / math.sqrt(HDIM)
FAR = 1e30
SLOTS = 16
STEP = 8
VMEM = pl.BlockSpec(memory_space=pltpu.VMEM)
SMEM = pl.BlockSpec(memory_space=pltpu.SMEM)
HBM = pl.BlockSpec(memory_space=pltpu.HBM)
LIMIT = pltpu.CompilerParams(vmem_limit_bytes=24 * 1024 * 1024)
F32 = jnp.float32
BF16 = jnp.bfloat16


def cost(flops):
    return pl.CostEstimate(flops=flops, bytes_accessed=1_000_000, transcendentals=0)


def split_kernel(*refs):
    count = len(refs) - 3
    sources, out_ref, held, sems = refs[:count], refs[count], refs[count + 1], refs[count + 2]
    copies = [pltpu.make_async_copy(ref, held.at[place], sems.at[place]) for place, ref in enumerate(sources)]
    for copy in copies:
        copy.start()
    for place, copy in enumerate(copies):
        copy.wait()
        for tile in range(TILES):
            turned = held[place, :, tile * BLK : (tile + 1) * BLK].T
            first = tile * BLK
            while first < (tile + 1) * BLK:
                part, row = divmod(first, WIDTH)
                size = min((tile + 1) * BLK - first, WIDTH - row)
                skip = first - tile * BLK
                out_ref[part, place * WIDTH + row : place * WIDTH + row + size, :] = turned[skip : skip + size, :]
                first += size


def split_heads(*arrays):
    count = len(arrays)
    return pl.pallas_call(
        split_kernel,
        out_shape=jax.ShapeDtypeStruct((PER, WIDTH * count, BLK), BF16),
        in_specs=[HBM] * count,
        out_specs=VMEM,
        scratch_shapes=[pltpu.VMEM((count, BLK, PER * WIDTH), BF16), pltpu.SemaphoreType.DMA((count,))],
        cost_estimate=cost(500_000_000 * count),
        name="split_heads",
    )(*arrays)


def join_kernel(in_ref, out_ref):
    out_ref[...] = in_ref[...].reshape(PER * WIDTH, BLK).T


def join_heads(parts):
    return pl.pallas_call(
        join_kernel,
        out_shape=jax.ShapeDtypeStruct((BLK, PER * WIDTH), BF16),
        in_specs=[VMEM],
        out_specs=VMEM,
        compiler_params=LIMIT,
        name="join_heads",
    )(parts)


def both_heads(query):
    row = lax.broadcasted_iota(jnp.int32, (WIDTH, BLK), 0)
    none = jnp.zeros_like(query)
    return jnp.concatenate((jnp.where(row < HDIM, query, none), jnp.where(row < HDIM, none, query)), axis=1)


def diagonal(total):
    return jnp.concatenate((total[:HDIM, :BLK], total[HDIM:, BLK:]), axis=0)


def per_row(stat):
    return jnp.concatenate(
        (
            jnp.broadcast_to(stat[:, :BLK], (HDIM, BLK)),
            jnp.broadcast_to(stat[:, BLK:], (HDIM, BLK)),
        ),
        axis=0,
    )


def own_kernel(image_ref, qkv_ref, out_ref, acc_ref, max_ref, den_ref, keys, scores):
    for block in range(PER):
        keys[block * BLK : (block + 1) * BLK, :] = qkv_ref[block, WIDTH : 2 * WIDTH, :].T

    group = lax.axis_index("sup") * PER

    def one(i, carry):
        image = image_ref[group + i]
        first = sum((image_ref[group + j] < image).astype(jnp.int32) for j in range(PER))
        last = sum((image_ref[group + j] <= image).astype(jnp.int32) for j in range(PER))
        weights_in = both_heads(qkv_ref[i, :WIDTH, :])
        top = jnp.full((1, 2 * BLK), -FAR, F32)
        for j in range(PER):
            rows = slice(j * BLK, (j + 1) * BLK)
            found = jnp.dot(keys[rows, :], weights_in, preferred_element_type=F32)
            scores[rows, :] = found
            inside = (j >= first) & (j < last)
            top = jnp.maximum(top, jnp.where(inside, jnp.max(found, axis=0, keepdims=True), -FAR))
        shift = top * SCALE_LOG2
        total = jnp.zeros((WIDTH, 2 * BLK), F32)
        den = jnp.zeros((1, 2 * BLK), F32)
        for j in range(PER):
            rows = slice(j * BLK, (j + 1) * BLK)
            inside = (j >= first) & (j < last)
            here = jnp.where(inside, shift, FAR)
            weights = jnp.exp2(scores[rows, :] * SCALE_LOG2 - here)
            den += jnp.sum(weights, axis=0, keepdims=True)
            total += jnp.dot(qkv_ref[j, 2 * WIDTH :, :], weights.astype(BF16), preferred_element_type=F32)
        acc = diagonal(total)
        acc_ref[i] = acc
        max_ref[i] = top
        den_ref[i] = den
        out_ref[i] = (acc * per_row(1.0 / den)).astype(BF16)
        return carry

    lax.fori_loop(0, PER, one, 0)


def own_part(image, qkv):
    return pl.pallas_call(
        own_kernel,
        out_shape=(
            jax.ShapeDtypeStruct((PER, WIDTH, BLK), BF16),
            jax.ShapeDtypeStruct((PER, WIDTH, BLK), F32),
            jax.ShapeDtypeStruct((PER, 1, 2 * BLK), F32),
            jax.ShapeDtypeStruct((PER, 1, 2 * BLK), F32),
        ),
        in_specs=[SMEM, VMEM],
        out_specs=(VMEM,) * 4,
        scratch_shapes=[pltpu.VMEM((PER * BLK, WIDTH), BF16), pltpu.VMEM((PER * BLK, 2 * BLK), F32)],
        compiler_params=LIMIT,
        cost_estimate=cost(100_000_000_000),
        name="own_part",
    )(image, qkv)


def fold_rows(values, how):
    return how(values.reshape(BLK // 8, 8, 2 * BLK), axis=0)


def halo_kernel(side, image_ref, kv_ref, q_ref, start_ref, acc_ref, max_ref, den_ref, out_ref, *scratch):
    keys, scores, tops, shifts, sums, dens = scratch
    place, places = lax.axis_index("sup"), lax.axis_size("sup")
    group = place * PER
    if side == 0:
        image, beyond = image_ref[group], jnp.maximum(group - (PER - 1), 0)
        there = place > 0
    else:
        image, beyond = image_ref[group + PER - 1], jnp.minimum(group + PER, (places - 1) * PER)
        there = place < places - 1
    count = sum((there & (image_ref[beyond + j] == image)).astype(jnp.int32) for j in range(PER - 1))
    queries = sum((image_ref[group + j] == image).astype(jnp.int32) for j in range(PER))
    pairs = count * queries
    first_query = 0 if side == 0 else PER - queries
    first_key = PER - 1 - count if side == 0 else 0
    steps = (pairs + STEP - 1) // STEP

    def advance(at):
        i, j = at
        wrap = j + 1 == count
        return jnp.where(wrap, jnp.minimum(i + 1, PER - 1), i), jnp.where(wrap, 0, j + 1)

    out_ref[...] = start_ref[...]

    @pl.when(pairs > 0)
    def _():
        for block in range(PER - 1):
            keys[block] = kv_ref[block, :WIDTH, :].T
        for block in range(PER):
            tops[block] = jnp.broadcast_to(max_ref[block], (8, 2 * BLK))

        def look(step, at):
            for lane in range(STEP):
                pair = step * STEP + lane
                i, j = at[0], first_key + at[1]
                at = advance(at)
                found = jnp.dot(keys[j], both_heads(q_ref[i, :WIDTH, :]), preferred_element_type=F32)
                scores[pair] = found
                tops[i] = jnp.maximum(tops[i], fold_rows(found, jnp.max))
            return at

        start = (jnp.int32(first_query), jnp.int32(0))
        lax.fori_loop(0, steps, look, start)
        for block in range(PER):
            shifts[block] = jnp.max(tops[block], axis=0, keepdims=True) * SCALE_LOG2
        sums[...] = jnp.zeros_like(sums)
        dens[...] = jnp.zeros_like(dens)

        def weigh(step, at):
            for lane in range(STEP):
                pair = step * STEP + lane
                i, j = at[0], first_key + at[1]
                at = advance(at)
                shift = jnp.where(pair < pairs, shifts[i], FAR)
                weights = jnp.exp2(scores[pair] * SCALE_LOG2 - shift)
                dens[i] += fold_rows(weights, jnp.sum)
                sums[i] += diagonal(jnp.dot(kv_ref[j, WIDTH:, :], weights.astype(BF16), preferred_element_type=F32))
            return at

        lax.fori_loop(0, steps, weigh, start)

        def close(i, carry):
            fade = jnp.exp2(max_ref[i] * SCALE_LOG2 - shifts[i])
            share = 1.0 / (den_ref[i] * fade + jnp.sum(dens[i], axis=0, keepdims=True))
            out_ref[i] = (acc_ref[i] * per_row(fade * share) + sums[i] * per_row(share)).astype(BF16)
            return carry

        lax.fori_loop(first_query, first_query + queries, close, 0)


def halo_part(side, image, kv, q, start, acc, top, den):
    return pl.pallas_call(
        functools.partial(halo_kernel, side),
        out_shape=jax.ShapeDtypeStruct((PER, WIDTH, BLK), BF16),
        in_specs=[SMEM] + [VMEM] * 6,
        out_specs=VMEM,
        scratch_shapes=[
            pltpu.VMEM((PER - 1, BLK, WIDTH), BF16),
            pltpu.VMEM((SLOTS, BLK, 2 * BLK), F32),
            pltpu.VMEM((PER, 8, 2 * BLK), F32),
            pltpu.VMEM((PER, 1, 2 * BLK), F32),
            pltpu.VMEM((PER, WIDTH, BLK), F32),
            pltpu.VMEM((PER, 8, 2 * BLK), F32),
        ],
        compiler_params=LIMIT,
        cost_estimate=cost(1_000_000_000),
        name="halo_part",
    )(image, kv, q, start, acc, top, den)


def shifted(value, steps):
    count = lax.axis_size("sup")
    pairs = [(i, i + steps) for i in range(count) if 0 <= i + steps < count]
    return lax.ppermute(value, "sup", pairs)


def regrouped(parts):
    return lax.all_to_all(parts, ("core", "grp"), 0, 0, tiled=True)


def body(query_rows, key_rows, value_rows, block_image):
    qkv = regrouped(split_heads(query_rows, key_rows, value_rows))
    rising = qkv[1:, WIDTH:]
    below = shifted(rising, 1)
    qkv, rising = lax.optimization_barrier((qkv, rising))
    above = shifted(qkv[:-1, WIDTH:], -1)
    start, acc, top, den = own_part(block_image, qkv)
    result = halo_part(0, block_image, below, qkv, start, acc, top, den)
    result = halo_part(1, block_image, above, qkv, result, acc, top, den)
    return join_heads(regrouped(result))


def solution(mesh):
    per_group = mesh.shape["grp"]
    cores = PER // per_group
    devices = mesh.devices.reshape(-1, cores, per_group)
    inner = jax.sharding.Mesh(devices, ("sup", "core", "grp"))
    rows = P(("sup", "core", "grp"), None)
    return jax.shard_map(
        body,
        mesh=inner,
        in_specs=(rows, rows, rows, P()),
        out_specs=rows,
        check_vma=False,
    )
```

```python
import functools
import math

import jax
import jax.numpy as jnp
from jax import lax
from jax.experimental import pallas as pl
from jax.experimental.pallas import tpu as pltpu
from jax.sharding import PartitionSpec as P

HDIM = 80
BLK = 128
PER = 8
HEADS_HERE = 2
WIDTH = HEADS_HERE * HDIM
TILES = PER * WIDTH // BLK
SCALE_LOG2 = math.log2(math.e) / math.sqrt(HDIM)
FAR = 1e30
SLOTS = 16
STEP = 8
VMEM = pl.BlockSpec(memory_space=pltpu.VMEM)
SMEM = pl.BlockSpec(memory_space=pltpu.SMEM)
HBM = pl.BlockSpec(memory_space=pltpu.HBM)
LIMIT = pltpu.CompilerParams(vmem_limit_bytes=24 * 1024 * 1024)
F32 = jnp.float32
BF16 = jnp.bfloat16


def cost(flops):
    return pl.CostEstimate(flops=flops, bytes_accessed=1_000_000, transcendentals=0)


def split_kernel(*refs):
    count = len(refs) - 3
    sources, out_ref, held, sems = refs[:count], refs[count], refs[count + 1], refs[count + 2]
    copies = [pltpu.make_async_copy(ref, held.at[place], sems.at[place]) for place, ref in enumerate(sources)]
    for copy in copies:
        copy.start()
    for place, copy in enumerate(copies):
        copy.wait()
        for tile in range(TILES):
            turned = held[place, :, tile * BLK : (tile + 1) * BLK].T
            first = tile * BLK
            while first < (tile + 1) * BLK:
                part, row = divmod(first, WIDTH)
                size = min((tile + 1) * BLK - first, WIDTH - row)
                skip = first - tile * BLK
                out_ref[part, place * WIDTH + row : place * WIDTH + row + size, :] = turned[skip : skip + size, :]
                first += size


def split_heads(*arrays):
    count = len(arrays)
    return pl.pallas_call(
        split_kernel,
        out_shape=jax.ShapeDtypeStruct((PER, WIDTH * count, BLK), BF16),
        in_specs=[HBM] * count,
        out_specs=VMEM,
        scratch_shapes=[pltpu.VMEM((count, BLK, PER * WIDTH), BF16), pltpu.SemaphoreType.DMA((count,))],
        cost_estimate=cost(500_000_000 * count),
        name="split_heads",
    )(*arrays)


def join_kernel(in_ref, out_ref):
    out_ref[...] = in_ref[...].reshape(PER * WIDTH, BLK).T


def join_heads(parts):
    return pl.pallas_call(
        join_kernel,
        out_shape=jax.ShapeDtypeStruct((BLK, PER * WIDTH), BF16),
        in_specs=[VMEM],
        out_specs=VMEM,
        compiler_params=LIMIT,
        name="join_heads",
    )(parts)


def both_heads(query):
    row = lax.broadcasted_iota(jnp.int32, (WIDTH, BLK), 0)
    none = jnp.zeros_like(query)
    return jnp.concatenate((jnp.where(row < HDIM, query, none), jnp.where(row < HDIM, none, query)), axis=1)


def diagonal(total):
    return jnp.concatenate((total[:HDIM, :BLK], total[HDIM:, BLK:]), axis=0)


def per_row(stat):
    return jnp.concatenate(
        (
            jnp.broadcast_to(stat[:, :BLK], (HDIM, BLK)),
            jnp.broadcast_to(stat[:, BLK:], (HDIM, BLK)),
        ),
        axis=0,
    )


def own_kernel(image_ref, qkv_ref, out_ref, acc_ref, max_ref, den_ref, keys, scores):
    for block in range(PER):
        keys[block * BLK : (block + 1) * BLK, :] = qkv_ref[block, WIDTH : 2 * WIDTH, :].T

    group = lax.axis_index("sup") * PER

    def one(i, carry):
        image = image_ref[group + i]
        first = sum((image_ref[group + j] < image).astype(jnp.int32) for j in range(PER))
        last = sum((image_ref[group + j] <= image).astype(jnp.int32) for j in range(PER))
        weights_in = both_heads(qkv_ref[i, :WIDTH, :])
        top = jnp.full((1, 2 * BLK), -FAR, F32)
        for j in range(PER):
            rows = slice(j * BLK, (j + 1) * BLK)
            found = jnp.dot(keys[rows, :], weights_in, preferred_element_type=F32)
            scores[rows, :] = found
            inside = (j >= first) & (j < last)
            top = jnp.maximum(top, jnp.where(inside, jnp.max(found, axis=0, keepdims=True), -FAR))
        shift = top * SCALE_LOG2
        total = jnp.zeros((WIDTH, 2 * BLK), F32)
        den = jnp.zeros((1, 2 * BLK), F32)
        for j in range(PER):
            rows = slice(j * BLK, (j + 1) * BLK)
            inside = (j >= first) & (j < last)
            here = jnp.where(inside, shift, FAR)
            weights = jnp.exp2(scores[rows, :] * SCALE_LOG2 - here)
            den += jnp.sum(weights, axis=0, keepdims=True)
            total += jnp.dot(qkv_ref[j, 2 * WIDTH :, :], weights.astype(BF16), preferred_element_type=F32)
        acc = diagonal(total)
        acc_ref[i] = acc
        max_ref[i] = top
        den_ref[i] = den
        out_ref[i] = (acc * per_row(1.0 / den)).astype(BF16)
        return carry

    lax.fori_loop(0, PER, one, 0)


def own_part(image, qkv):
    return pl.pallas_call(
        own_kernel,
        out_shape=(
            jax.ShapeDtypeStruct((PER, WIDTH, BLK), BF16),
            jax.ShapeDtypeStruct((PER, WIDTH, BLK), F32),
            jax.ShapeDtypeStruct((PER, 1, 2 * BLK), F32),
            jax.ShapeDtypeStruct((PER, 1, 2 * BLK), F32),
        ),
        in_specs=[SMEM, VMEM],
        out_specs=(VMEM,) * 4,
        scratch_shapes=[pltpu.VMEM((PER * BLK, WIDTH), BF16), pltpu.VMEM((PER * BLK, 2 * BLK), F32)],
        compiler_params=LIMIT,
        cost_estimate=cost(100_000_000_000),
        name="own_part",
    )(image, qkv)


def fold_rows(values, how):
    return how(values.reshape(BLK // 8, 8, 2 * BLK), axis=0)


def halo_kernel(turn, image_ref, kv_ref, q_ref, start_ref, acc_ref, max_ref, den_ref, out_ref, *scratch):
    keys, scores, tops, shifts, sums, dens = scratch
    place, places = lax.axis_index("sup"), lax.axis_size("sup")
    from_below = lax.axis_index("core") == turn
    group = place * PER
    image = image_ref[jnp.where(from_below, group, group + PER - 1)]
    beyond = jnp.where(
        from_below, jnp.maximum(group - (PER - 1), 0), jnp.minimum(group + PER, (places - 1) * PER)
    )
    there = jnp.where(from_below, place > 0, place < places - 1)
    count = sum((there & (image_ref[beyond + j] == image)).astype(jnp.int32) for j in range(PER - 1))
    queries = sum((image_ref[group + j] == image).astype(jnp.int32) for j in range(PER))
    pairs = count * queries
    first_query = jnp.where(from_below, 0, PER - queries)
    first_key = jnp.where(from_below, PER - 1 - count, 0)
    steps = (pairs + STEP - 1) // STEP

    def advance(at):
        i, j = at
        wrap = j + 1 == count
        return jnp.where(wrap, jnp.minimum(i + 1, PER - 1), i), jnp.where(wrap, 0, j + 1)

    out_ref[...] = start_ref[...]

    @pl.when(pairs > 0)
    def _():
        for block in range(PER - 1):
            keys[block] = kv_ref[block, :WIDTH, :].T
        for block in range(PER):
            tops[block] = jnp.broadcast_to(max_ref[block], (8, 2 * BLK))

        def look(step, at):
            for lane in range(STEP):
                pair = step * STEP + lane
                i, j = at[0], first_key + at[1]
                at = advance(at)
                found = jnp.dot(keys[j], both_heads(q_ref[i, :WIDTH, :]), preferred_element_type=F32)
                scores[pair] = found
                tops[i] = jnp.maximum(tops[i], fold_rows(found, jnp.max))
            return at

        start = (first_query, jnp.int32(0))
        lax.fori_loop(0, steps, look, start)
        for block in range(PER):
            shifts[block] = jnp.max(tops[block], axis=0, keepdims=True) * SCALE_LOG2
        sums[...] = jnp.zeros_like(sums)
        dens[...] = jnp.zeros_like(dens)

        def weigh(step, at):
            for lane in range(STEP):
                pair = step * STEP + lane
                i, j = at[0], first_key + at[1]
                at = advance(at)
                shift = jnp.where(pair < pairs, shifts[i], FAR)
                weights = jnp.exp2(scores[pair] * SCALE_LOG2 - shift)
                dens[i] += fold_rows(weights, jnp.sum)
                sums[i] += diagonal(jnp.dot(kv_ref[j, WIDTH:, :], weights.astype(BF16), preferred_element_type=F32))
            return at

        lax.fori_loop(0, steps, weigh, start)

        def close(i, carry):
            fade = jnp.exp2(max_ref[i] * SCALE_LOG2 - shifts[i])
            share = 1.0 / (den_ref[i] * fade + jnp.sum(dens[i], axis=0, keepdims=True))
            out_ref[i] = (acc_ref[i] * per_row(fade * share) + sums[i] * per_row(share)).astype(BF16)
            return carry

        lax.fori_loop(first_query, first_query + queries, close, 0)


def halo_part(turn, image, kv, q, start, acc, top, den):
    return pl.pallas_call(
        functools.partial(halo_kernel, turn),
        out_shape=jax.ShapeDtypeStruct((PER, WIDTH, BLK), BF16),
        in_specs=[SMEM] + [VMEM] * 6,
        out_specs=VMEM,
        scratch_shapes=[
            pltpu.VMEM((PER - 1, BLK, WIDTH), BF16),
            pltpu.VMEM((SLOTS, BLK, 2 * BLK), F32),
            pltpu.VMEM((PER, 8, 2 * BLK), F32),
            pltpu.VMEM((PER, 1, 2 * BLK), F32),
            pltpu.VMEM((PER, WIDTH, BLK), F32),
            pltpu.VMEM((PER, 8, 2 * BLK), F32),
        ],
        compiler_params=LIMIT,
        cost_estimate=cost(1_000_000_000),
        name="halo_part",
    )(image, kv, q, start, acc, top, den)


def exchanged(qkv, turn):
    groups, cores = lax.axis_size("sup"), lax.axis_size("core")
    pairs = []
    for core in range(cores):
        step = 1 if core == turn else -1
        pairs += [
            (group * cores + core, (group + step) * cores + core)
            for group in range(groups)
            if 0 <= group + step < groups
        ]
    first = (lax.axis_index("core") == turn).astype(jnp.int32)
    part = lax.dynamic_slice(qkv, (first, WIDTH, 0), (PER - 1, 2 * WIDTH, BLK))
    return part, lax.ppermute(part, ("sup", "core"), pairs)


def regrouped(parts):
    return lax.all_to_all(parts, ("core", "grp"), 0, 0, tiled=True)


def body(query_rows, key_rows, value_rows, block_image):
    qkv = regrouped(split_heads(query_rows, key_rows, value_rows))
    part, near = exchanged(qkv, 0)
    again, part = lax.optimization_barrier((qkv, part))
    part, far = exchanged(again, 1)
    start, acc, top, den = own_part(block_image, qkv)
    result = halo_part(0, block_image, near, qkv, start, acc, top, den)
    result = halo_part(1, block_image, far, qkv, result, acc, top, den)
    return join_heads(regrouped(result))


def solution(mesh):
    per_group = mesh.shape["grp"]
    cores = PER // per_group
    devices = mesh.devices.reshape(-1, cores, per_group)
    inner = jax.sharding.Mesh(devices, ("sup", "core", "grp"))
    rows = P(("sup", "core", "grp"), None)
    return jax.shard_map(
        body,
        mesh=inner,
        in_specs=(rows, rows, rows, P()),
        out_specs=rows,
        check_vma=False,
    )
```

```python
import functools
import math

import jax
import jax.numpy as jnp
from jax import lax
from jax.experimental import pallas as pl
from jax.experimental.pallas import tpu as pltpu
from jax.sharding import PartitionSpec as P

HDIM = 80
BLK = 128
PER = 8
HEADS_HERE = 2
WIDTH = HEADS_HERE * HDIM
TILES = PER * WIDTH // BLK
SCALE_LOG2 = math.log2(math.e) / math.sqrt(HDIM)
FAR = 1e30
SLOTS = 16
STEP = 8
VMEM = pl.BlockSpec(memory_space=pltpu.VMEM)
SMEM = pl.BlockSpec(memory_space=pltpu.SMEM)
HBM = pl.BlockSpec(memory_space=pltpu.HBM)
LIMIT = pltpu.CompilerParams(vmem_limit_bytes=24 * 1024 * 1024)
F32 = jnp.float32
BF16 = jnp.bfloat16


def cost(flops):
    return pl.CostEstimate(flops=flops, bytes_accessed=1_000_000, transcendentals=0)


def split_kernel(*refs):
    count = len(refs) - 3
    sources, out_ref, held, sems = refs[:count], refs[count], refs[count + 1], refs[count + 2]
    copies = [pltpu.make_async_copy(ref, held.at[place], sems.at[place]) for place, ref in enumerate(sources)]
    for copy in copies:
        copy.start()
    for place, copy in enumerate(copies):
        copy.wait()
        for tile in range(TILES):
            turned = held[place, :, tile * BLK : (tile + 1) * BLK].T
            first = tile * BLK
            while first < (tile + 1) * BLK:
                part, row = divmod(first, WIDTH)
                size = min((tile + 1) * BLK - first, WIDTH - row)
                skip = first - tile * BLK
                out_ref[part, place * WIDTH + row : place * WIDTH + row + size, :] = turned[skip : skip + size, :]
                first += size


def split_heads(*arrays):
    count = len(arrays)
    return pl.pallas_call(
        split_kernel,
        out_shape=jax.ShapeDtypeStruct((PER, WIDTH * count, BLK), BF16),
        in_specs=[HBM] * count,
        out_specs=VMEM,
        scratch_shapes=[pltpu.VMEM((count, BLK, PER * WIDTH), BF16), pltpu.SemaphoreType.DMA((count,))],
        compiler_params=pltpu.CompilerParams(vmem_limit_bytes=49152 * 1024),
        cost_estimate=cost(500_000_000 * count),
        name="split_heads",
    )(*[pltpu.with_memory_space_constraint(a, pltpu.HBM) for a in arrays])


def join_kernel(in_ref, out_ref):
    out_ref[...] = in_ref[...].reshape(PER * WIDTH, BLK).T


def join_heads(parts):
    return pl.pallas_call(
        join_kernel,
        out_shape=jax.ShapeDtypeStruct((BLK, PER * WIDTH), BF16),
        in_specs=[VMEM],
        out_specs=VMEM,
        compiler_params=LIMIT,
        name="join_heads",
    )(parts)


def both_heads(query):
    row = lax.broadcasted_iota(jnp.int32, (WIDTH, BLK), 0)
    none = jnp.zeros_like(query)
    return jnp.concatenate((jnp.where(row < HDIM, query, none), jnp.where(row < HDIM, none, query)), axis=1)


def diagonal(total):
    return jnp.concatenate((total[:HDIM, :BLK], total[HDIM:, BLK:]), axis=0)


def per_row(stat):
    return jnp.concatenate(
        (
            jnp.broadcast_to(stat[:, :BLK], (HDIM, BLK)),
            jnp.broadcast_to(stat[:, BLK:], (HDIM, BLK)),
        ),
        axis=0,
    )


def own_kernel(image_ref, qkv_ref, out_ref, acc_ref, max_ref, den_ref, keys, scores):
    for block in range(PER):
        keys[block * BLK : (block + 1) * BLK, :] = qkv_ref[block, WIDTH : 2 * WIDTH, :].T

    group = lax.axis_index("sup") * PER

    def one(i, carry):
        image = image_ref[group + i]
        first = sum((image_ref[group + j] < image).astype(jnp.int32) for j in range(PER))
        last = sum((image_ref[group + j] <= image).astype(jnp.int32) for j in range(PER))
        weights_in = both_heads(qkv_ref[i, :WIDTH, :])
        top = jnp.full((1, 2 * BLK), -FAR, F32)
        for j in range(PER):
            rows = slice(j * BLK, (j + 1) * BLK)
            found = jnp.dot(keys[rows, :], weights_in, preferred_element_type=F32)
            scores[rows, :] = found
            inside = (j >= first) & (j < last)
            top = jnp.maximum(top, jnp.where(inside, jnp.max(found, axis=0, keepdims=True), -FAR))
        shift = top * SCALE_LOG2
        total = jnp.zeros((WIDTH, 2 * BLK), F32)
        den = jnp.zeros((1, 2 * BLK), F32)
        for j in range(PER):
            rows = slice(j * BLK, (j + 1) * BLK)
            inside = (j >= first) & (j < last)
            here = jnp.where(inside, shift, FAR)
            weights = jnp.exp2(scores[rows, :] * SCALE_LOG2 - here)
            den += jnp.sum(weights, axis=0, keepdims=True)
            total += jnp.dot(qkv_ref[j, 2 * WIDTH :, :], weights.astype(BF16), preferred_element_type=F32)
        acc = diagonal(total)
        acc_ref[i] = acc
        max_ref[i] = top
        den_ref[i] = den
        out_ref[i] = (acc * per_row(1.0 / den)).astype(BF16)
        return carry

    lax.fori_loop(0, PER, one, 0)


def own_part(image, qkv):
    return pl.pallas_call(
        own_kernel,
        out_shape=(
            jax.ShapeDtypeStruct((PER, WIDTH, BLK), BF16),
            jax.ShapeDtypeStruct((PER, WIDTH, BLK), F32),
            jax.ShapeDtypeStruct((PER, 1, 2 * BLK), F32),
            jax.ShapeDtypeStruct((PER, 1, 2 * BLK), F32),
        ),
        in_specs=[SMEM, VMEM],
        out_specs=(VMEM,) * 4,
        scratch_shapes=[pltpu.VMEM((PER * BLK, WIDTH), BF16), pltpu.VMEM((PER * BLK, 2 * BLK), F32)],
        compiler_params=LIMIT,
        cost_estimate=cost(100_000_000_000),
        name="own_part",
    )(image, qkv)


def fold_rows(values, how):
    return how(values.reshape(BLK // 8, 8, 2 * BLK), axis=0)


def halo_kernel(turn, image_ref, kv_ref, q_ref, start_ref, acc_ref, max_ref, den_ref, out_ref, *scratch):
    keys, scores, tops, shifts, sums, dens = scratch
    place, places = lax.axis_index("sup"), lax.axis_size("sup")
    from_below = lax.axis_index("core") == turn
    group = place * PER
    image = image_ref[jnp.where(from_below, group, group + PER - 1)]
    beyond = jnp.where(
        from_below, jnp.maximum(group - (PER - 1), 0), jnp.minimum(group + PER, (places - 1) * PER)
    )
    there = jnp.where(from_below, place > 0, place < places - 1)
    count = sum((there & (image_ref[beyond + j] == image)).astype(jnp.int32) for j in range(PER - 1))
    queries = sum((image_ref[group + j] == image).astype(jnp.int32) for j in range(PER))
    pairs = count * queries
    first_query = jnp.where(from_below, 0, PER - queries)
    first_key = jnp.where(from_below, PER - 1 - count, 0)
    steps = (pairs + STEP - 1) // STEP

    def advance(at):
        i, j = at
        wrap = j + 1 == count
        return jnp.where(wrap, jnp.minimum(i + 1, PER - 1), i), jnp.where(wrap, 0, j + 1)

    out_ref[...] = start_ref[...]

    @pl.when(pairs > 0)
    def _():
        for block in range(PER - 1):
            keys[block] = kv_ref[block, :WIDTH, :].T
        for block in range(PER):
            tops[block] = jnp.broadcast_to(max_ref[block], (8, 2 * BLK))

        def look(step, at):
            for lane in range(STEP):
                pair = step * STEP + lane
                i, j = at[0], first_key + at[1]
                at = advance(at)
                found = jnp.dot(keys[j], both_heads(q_ref[i, :WIDTH, :]), preferred_element_type=F32)
                scores[pair] = found
                tops[i] = jnp.maximum(tops[i], fold_rows(found, jnp.max))
            return at

        start = (first_query, jnp.int32(0))
        lax.fori_loop(0, steps, look, start)
        for block in range(PER):
            shifts[block] = jnp.max(tops[block], axis=0, keepdims=True) * SCALE_LOG2
        sums[...] = jnp.zeros_like(sums)
        dens[...] = jnp.zeros_like(dens)

        def weigh(step, at):
            for lane in range(STEP):
                pair = step * STEP + lane
                i, j = at[0], first_key + at[1]
                at = advance(at)
                shift = jnp.where(pair < pairs, shifts[i], FAR)
                weights = jnp.exp2(scores[pair] * SCALE_LOG2 - shift)
                dens[i] += fold_rows(weights, jnp.sum)
                sums[i] += diagonal(jnp.dot(kv_ref[j, WIDTH:, :], weights.astype(BF16), preferred_element_type=F32))
            return at

        lax.fori_loop(0, steps, weigh, start)

        def close(i, carry):
            fade = jnp.exp2(max_ref[i] * SCALE_LOG2 - shifts[i])
            share = 1.0 / (den_ref[i] * fade + jnp.sum(dens[i], axis=0, keepdims=True))
            out_ref[i] = (acc_ref[i] * per_row(fade * share) + sums[i] * per_row(share)).astype(BF16)
            return carry

        lax.fori_loop(first_query, first_query + queries, close, 0)


def halo_part(turn, image, kv, q, start, acc, top, den):
    return pl.pallas_call(
        functools.partial(halo_kernel, turn),
        out_shape=jax.ShapeDtypeStruct((PER, WIDTH, BLK), BF16),
        in_specs=[SMEM] + [VMEM] * 6,
        out_specs=VMEM,
        scratch_shapes=[
            pltpu.VMEM((PER - 1, BLK, WIDTH), BF16),
            pltpu.VMEM((SLOTS, BLK, 2 * BLK), F32),
            pltpu.VMEM((PER, 8, 2 * BLK), F32),
            pltpu.VMEM((PER, 1, 2 * BLK), F32),
            pltpu.VMEM((PER, WIDTH, BLK), F32),
            pltpu.VMEM((PER, 8, 2 * BLK), F32),
        ],
        compiler_params=LIMIT,
        cost_estimate=cost(1_000_000_000),
        name="halo_part",
    )(image, kv, q, start, acc, top, den)


def pick_kernel(turn, qkv_ref, out_ref):
    first = (lax.axis_index("core") == turn).astype(jnp.int32)
    out_ref[...] = qkv_ref[pl.ds(first, PER - 1), WIDTH:, :]


def picked(qkv, turn):
    return pl.pallas_call(
        functools.partial(pick_kernel, turn),
        out_shape=jax.ShapeDtypeStruct((PER - 1, 2 * WIDTH, BLK), BF16),
        in_specs=[VMEM],
        out_specs=VMEM,
        compiler_params=LIMIT,
        cost_estimate=cost(1_000_000),
        name="picked",
    )(qkv)


def exchanged(qkv, turn):
    groups, cores = lax.axis_size("sup"), lax.axis_size("core")
    pairs = []
    for core in range(cores):
        step = 1 if core == turn else -1
        pairs += [
            (group * cores + core, (group + step) * cores + core)
            for group in range(groups)
            if 0 <= group + step < groups
        ]
    part = picked(qkv, turn)
    return part, lax.ppermute(part, ("sup", "core"), pairs)


def regrouped(parts):
    return lax.all_to_all(parts, ("core", "grp"), 0, 0, tiled=True)


def body(query_rows, key_rows, value_rows, block_image):
    qkv = regrouped(split_heads(query_rows, key_rows, value_rows))
    part, near = exchanged(qkv, 0)
    again, part = lax.optimization_barrier((qkv, part))
    part, far = exchanged(again, 1)
    start, acc, top, den = own_part(block_image, qkv)
    result = halo_part(0, block_image, near, qkv, start, acc, top, den)
    result = halo_part(1, block_image, far, qkv, result, acc, top, den)
    return join_heads(regrouped(result))


def solution(mesh):
    per_group = mesh.shape["grp"]
    cores = PER // per_group
    devices = mesh.devices.reshape(-1, cores, per_group)
    inner = jax.sharding.Mesh(devices, ("sup", "core", "grp"))
    rows = P(("sup", "core", "grp"), None)
    return jax.shard_map(
        body,
        mesh=inner,
        in_specs=(rows, rows, rows, P()),
        out_specs=rows,
        check_vma=False,
    )
```

```python
import functools
import math

import jax
import jax.numpy as jnp
from jax import lax
from jax.experimental import pallas as pl
from jax.experimental.pallas import tpu as pltpu
from jax.sharding import PartitionSpec as P

HDIM = 80
BLK = 128
PER = 8
HEADS_HERE = 2
WIDTH = HEADS_HERE * HDIM
TILES = PER * WIDTH // BLK
SCALE_LOG2 = math.log2(math.e) / math.sqrt(HDIM)
FAR = 1e30
SLOTS = 16
STEP = 8
RUN = 16
VMEM = pl.BlockSpec(memory_space=pltpu.VMEM)
SMEM = pl.BlockSpec(memory_space=pltpu.SMEM)
HBM = pl.BlockSpec(memory_space=pltpu.HBM)
LIMIT = pltpu.CompilerParams(vmem_limit_bytes=24 * 1024 * 1024)
F32 = jnp.float32
BF16 = jnp.bfloat16


def cost(flops):
    return pl.CostEstimate(flops=flops, bytes_accessed=1_000_000, transcendentals=0)


def split_kernel(counts, *refs):
    count, outs = sum(counts), len(counts)
    sources, out_refs, (held, sems) = refs[:count], refs[count : count + outs], refs[count + outs :]
    copies = [pltpu.make_async_copy(ref, held.at[place], sems.at[place]) for place, ref in enumerate(sources)]
    for copy in copies:
        copy.start()
    places = [(out_ref, place) for out_ref, many in zip(out_refs, counts) for place in range(many)]
    for source, (out_ref, place) in enumerate(places):
        copies[source].wait()
        for tile in range(TILES):
            turned = held[source, :, tile * BLK : (tile + 1) * BLK].T
            first = tile * BLK
            while first < (tile + 1) * BLK:
                part, row = divmod(first, WIDTH)
                size = min((tile + 1) * BLK - first, WIDTH - row)
                skip = first - tile * BLK
                out_ref[part, place * WIDTH + row : place * WIDTH + row + size, :] = turned[skip : skip + size, :]
                first += size


def split_heads(*groups):
    arrays = [pltpu.with_memory_space_constraint(array, pltpu.HBM) for group in groups for array in group]
    counts = tuple(len(group) for group in groups)
    return pl.pallas_call(
        functools.partial(split_kernel, counts),
        out_shape=[jax.ShapeDtypeStruct((PER, WIDTH * count, BLK), BF16) for count in counts],
        in_specs=[HBM] * len(arrays),
        out_specs=[VMEM] * len(counts),
        scratch_shapes=[
            pltpu.VMEM((len(arrays), BLK, PER * WIDTH), BF16),
            pltpu.SemaphoreType.DMA((len(arrays),)),
        ],
        compiler_params=pltpu.CompilerParams(vmem_limit_bytes=49152 * 1024),
        cost_estimate=cost(500_000_000 * len(arrays)),
        name="split_heads",
    )(*arrays)


def join_kernel(in_ref, out_ref):
    out_ref[...] = in_ref[...].reshape(PER * WIDTH, BLK).T


def join_heads(parts):
    return pl.pallas_call(
        join_kernel,
        out_shape=jax.ShapeDtypeStruct((BLK, PER * WIDTH), BF16),
        in_specs=[VMEM],
        out_specs=VMEM,
        compiler_params=LIMIT,
        name="join_heads",
    )(parts)


def both_heads(query):
    row = lax.broadcasted_iota(jnp.int32, (WIDTH, BLK), 0)
    none = jnp.zeros_like(query)
    return jnp.concatenate((jnp.where(row < HDIM, query, none), jnp.where(row < HDIM, none, query)), axis=1)


def diagonal(total):
    return jnp.concatenate((total[:HDIM, :BLK], total[HDIM:, BLK:]), axis=0)


def per_row(stat):
    return jnp.concatenate(
        (
            jnp.broadcast_to(stat[:, :BLK], (HDIM, BLK)),
            jnp.broadcast_to(stat[:, BLK:], (HDIM, BLK)),
        ),
        axis=0,
    )


def fold_rows(values, how):
    return how(values.reshape(BLK // 8, 8, 2 * BLK), axis=0)


def own_kernel(image_ref, kv_ref, q_ref, out_ref, acc_ref, max_ref, den_ref, *scratch):
    bounds, keys, scores, tops, shifts, dens = scratch
    group = lax.axis_index("sup") * PER
    pairs = jnp.int32(0)
    for block in range(PER):
        image = image_ref[group + block]
        first = sum((image_ref[group + j] < image).astype(jnp.int32) for j in range(PER))
        last = sum((image_ref[group + j] <= image).astype(jnp.int32) for j in range(PER))
        bounds[0, block] = first
        bounds[1, block] = last
        pairs += last - first
        keys[block] = kv_ref[block, :WIDTH, :].T
    steps = (pairs + STEP - 1) // STEP
    tops[...] = jnp.full_like(tops, -FAR)
    dens[...] = jnp.zeros_like(dens)
    acc_ref[...] = jnp.zeros_like(acc_ref)

    def advance(at):
        i, j = at
        wrap = j + 1 == bounds[1, i]
        i = jnp.where(wrap, jnp.minimum(i + 1, PER - 1), i)
        return i, jnp.where(wrap, bounds[0, i], j + 1)

    def look(step, at):
        for lane in range(STEP):
            i, j = at
            at = advance(at)
            found = jnp.dot(keys[j], both_heads(q_ref[i]), preferred_element_type=F32)
            scores[step * STEP + lane] = found
            tops[i] = jnp.maximum(tops[i], fold_rows(found, jnp.max))
        return at

    start = (jnp.int32(0), jnp.int32(0))
    lax.fori_loop(0, steps, look, start)
    for block in range(PER):
        top = jnp.max(tops[block], axis=0, keepdims=True)
        max_ref[block] = top
        shifts[block] = top * SCALE_LOG2

    def weigh(step, at):
        for lane in range(STEP):
            pair = step * STEP + lane
            i, j = at
            at = advance(at)
            shift = jnp.where(pair < pairs, shifts[i], FAR)
            weights = jnp.exp2(scores[pair] * SCALE_LOG2 - shift)
            dens[i] += fold_rows(weights, jnp.sum)
            acc_ref[i] += diagonal(jnp.dot(kv_ref[j, WIDTH:, :], weights.astype(BF16), preferred_element_type=F32))
        return at

    lax.fori_loop(0, steps, weigh, start)
    for block in range(PER):
        den = jnp.sum(dens[block], axis=0, keepdims=True)
        den_ref[block] = den
        out_ref[block] = (acc_ref[block] * per_row(1.0 / den)).astype(BF16)


def own_part(image, kv, q):
    return pl.pallas_call(
        own_kernel,
        out_shape=(
            jax.ShapeDtypeStruct((PER, WIDTH, BLK), BF16),
            jax.ShapeDtypeStruct((PER, WIDTH, BLK), F32),
            jax.ShapeDtypeStruct((PER, 1, 2 * BLK), F32),
            jax.ShapeDtypeStruct((PER, 1, 2 * BLK), F32),
        ),
        in_specs=[SMEM, VMEM, VMEM],
        out_specs=(VMEM,) * 4,
        scratch_shapes=[
            pltpu.SMEM((2, PER), jnp.int32),
            pltpu.VMEM((PER, BLK, WIDTH), BF16),
            pltpu.VMEM((PER * PER, BLK, 2 * BLK), F32),
            pltpu.VMEM((PER, 8, 2 * BLK), F32),
            pltpu.VMEM((PER, 1, 2 * BLK), F32),
            pltpu.VMEM((PER, 8, 2 * BLK), F32),
        ],
        compiler_params=LIMIT,
        cost_estimate=cost(100_000_000_000),
        name="own_part",
    )(image, kv, q)


def halo_kernel(turn, image_ref, kv_ref, q_ref, start_ref, acc_ref, max_ref, den_ref, out_ref, *scratch):
    keys, scores, tops, shifts, sums, dens = scratch
    place, places = lax.axis_index("sup"), lax.axis_size("sup")
    from_below = lax.axis_index("core") == turn
    group = place * PER
    image = image_ref[jnp.where(from_below, group, group + PER - 1)]
    beyond = jnp.where(
        from_below, jnp.maximum(group - (PER - 1), 0), jnp.minimum(group + PER, (places - 1) * PER)
    )
    there = jnp.where(from_below, place > 0, place < places - 1)
    count = sum((there & (image_ref[beyond + j] == image)).astype(jnp.int32) for j in range(PER - 1))
    queries = sum((image_ref[group + j] == image).astype(jnp.int32) for j in range(PER))
    pairs = count * queries
    first_query = jnp.where(from_below, 0, PER - queries)
    first_key = jnp.where(from_below, PER - 1 - count, 0)
    steps = (pairs + STEP - 1) // STEP

    def advance(at):
        i, j = at
        wrap = j + 1 == count
        return jnp.where(wrap, jnp.minimum(i + 1, PER - 1), i), jnp.where(wrap, 0, j + 1)

    out_ref[...] = start_ref[...]

    @pl.when(pairs > 0)
    def _():
        for block in range(PER - 1):
            keys[block] = kv_ref[block, :WIDTH, :].T
        for block in range(PER):
            tops[block] = jnp.broadcast_to(max_ref[block], (8, 2 * BLK))

        def look(step, at):
            for lane in range(STEP):
                pair = step * STEP + lane
                i, j = at[0], first_key + at[1]
                at = advance(at)
                found = jnp.dot(keys[j], both_heads(q_ref[i]), preferred_element_type=F32)
                scores[pair] = found
                tops[i] = jnp.maximum(tops[i], fold_rows(found, jnp.max))
            return at

        start = (first_query, jnp.int32(0))
        lax.fori_loop(0, steps, look, start)
        for block in range(PER):
            shifts[block] = jnp.max(tops[block], axis=0, keepdims=True) * SCALE_LOG2
        sums[...] = jnp.zeros_like(sums)
        dens[...] = jnp.zeros_like(dens)

        def weigh(step, at):
            for lane in range(STEP):
                pair = step * STEP + lane
                i, j = at[0], first_key + at[1]
                at = advance(at)
                shift = jnp.where(pair < pairs, shifts[i], FAR)
                weights = jnp.exp2(scores[pair] * SCALE_LOG2 - shift)
                dens[i] += fold_rows(weights, jnp.sum)
                sums[i] += diagonal(jnp.dot(kv_ref[j, WIDTH:, :], weights.astype(BF16), preferred_element_type=F32))
            return at

        lax.fori_loop(0, steps, weigh, start)

        def close(i, carry):
            fade = jnp.exp2(max_ref[i] * SCALE_LOG2 - shifts[i])
            share = 1.0 / (den_ref[i] * fade + jnp.sum(dens[i], axis=0, keepdims=True))
            out_ref[i] = (acc_ref[i] * per_row(fade * share) + sums[i] * per_row(share)).astype(BF16)
            return carry

        lax.fori_loop(first_query, first_query + queries, close, 0)


def halo_part(turn, image, kv, q, start, acc, top, den):
    return pl.pallas_call(
        functools.partial(halo_kernel, turn),
        out_shape=jax.ShapeDtypeStruct((PER, WIDTH, BLK), BF16),
        in_specs=[SMEM] + [VMEM] * 6,
        out_specs=VMEM,
        scratch_shapes=[
            pltpu.VMEM((PER - 1, BLK, WIDTH), BF16),
            pltpu.VMEM((SLOTS, BLK, 2 * BLK), F32),
            pltpu.VMEM((PER, 8, 2 * BLK), F32),
            pltpu.VMEM((PER, 1, 2 * BLK), F32),
            pltpu.VMEM((PER, WIDTH, BLK), F32),
            pltpu.VMEM((PER, 8, 2 * BLK), F32),
        ],
        compiler_params=LIMIT,
        cost_estimate=cost(1_000_000_000),
        name="halo_part",
    )(image, kv, q, start, acc, top, den)


def pick_kernel(turn, kv_ref, out_ref):
    first = (lax.axis_index("core") == turn).astype(jnp.int32)
    out_ref[...] = kv_ref[pl.ds(first, PER - 1)]


def picked(kv, turn):
    return pl.pallas_call(
        functools.partial(pick_kernel, turn),
        out_shape=jax.ShapeDtypeStruct((PER - 1, 2 * WIDTH, BLK), BF16),
        in_specs=[VMEM],
        out_specs=VMEM,
        compiler_params=LIMIT,
        cost_estimate=cost(1_000_000),
        name="picked",
    )(kv)


def exchanged(kv, turn):
    groups, cores = lax.axis_size("sup"), lax.axis_size("core")
    pairs = []
    for core in range(cores):
        step = 1 if core == turn else -1
        pairs += [
            (group * cores + core, (group + step) * cores + core)
            for group in range(groups)
            if 0 <= group + step < groups
        ]
    part = picked(kv, turn)
    return part, lax.ppermute(part, ("sup", "core"), pairs)


def regrouped(parts):
    return lax.all_to_all(parts, ("core", "grp"), 0, 0, tiled=True)


def body(query_rows, key_rows, value_rows, block_image):
    late = lax.rem(lax.axis_index("sup"), RUN) == RUN - 1

    def together(query_rows, key_rows, value_rows):
        (slabs,) = split_heads((query_rows, key_rows, value_rows))
        qkv = regrouped(slabs)
        return qkv[:, WIDTH:], qkv[:, :WIDTH]

    def keys_first(query_rows, key_rows, value_rows):
        slabs, q = split_heads((key_rows, value_rows), (query_rows,))
        return regrouped(slabs), q

    kv, q = lax.cond(late, keys_first, together, query_rows, key_rows, value_rows)
    part, near = exchanged(kv, 0)
    again, part = lax.optimization_barrier((kv, part))
    part, far = exchanged(again, 1)
    part, q = lax.optimization_barrier((part, q))
    q = lax.cond(late, regrouped, lambda q: q, q)
    start, acc, top, den = own_part(block_image, kv, q)
    result = halo_part(0, block_image, near, q, start, acc, top, den)
    result = halo_part(1, block_image, far, q, result, acc, top, den)
    return join_heads(regrouped(result))


def solution(mesh):
    per_group = mesh.shape["grp"]
    cores = PER // per_group
    devices = mesh.devices.reshape(-1, cores, per_group)
    inner = jax.sharding.Mesh(devices, ("sup", "core", "grp"))
    rows = P(("sup", "core", "grp"), None)
    return jax.shard_map(
        body,
        mesh=inner,
        in_specs=(rows, rows, rows, P()),
        out_specs=rows,
        check_vma=False,
    )
```

```python
import functools
import math

import jax
import jax.numpy as jnp
from jax import lax
from jax.experimental import pallas as pl
from jax.experimental.pallas import tpu as pltpu
from jax.sharding import PartitionSpec as P

HDIM = 80
BLK = 128
PER = 8
HEADS_HERE = 2
WIDTH = HEADS_HERE * HDIM
TILES = PER * WIDTH // BLK
SCALE_LOG2 = math.log2(math.e) / math.sqrt(HDIM)
FAR = 1e30
SLOTS = 16
STEP = 8
RUN = 16
FEW = 4
VMEM = pl.BlockSpec(memory_space=pltpu.VMEM)
SMEM = pl.BlockSpec(memory_space=pltpu.SMEM)
HBM = pl.BlockSpec(memory_space=pltpu.HBM)
LIMIT = pltpu.CompilerParams(vmem_limit_bytes=24 * 1024 * 1024)
F32 = jnp.float32
BF16 = jnp.bfloat16


def cost(flops):
    return pl.CostEstimate(flops=flops, bytes_accessed=1_000_000, transcendentals=0)


def is_late():
    return lax.rem(lax.axis_index("sup"), RUN) >= FEW


def split_kernel(counts, *refs):
    count, outs = sum(counts), len(counts)
    sources, out_refs, (held, sems) = refs[:count], refs[count : count + outs], refs[count + outs :]
    copies = [pltpu.make_async_copy(ref, held.at[place], sems.at[place]) for place, ref in enumerate(sources)]
    for copy in copies:
        copy.start()
    places = [(out_ref, place) for out_ref, many in zip(out_refs, counts) for place in range(many)]
    for source, (out_ref, place) in enumerate(places):
        copies[source].wait()
        for tile in range(TILES):
            turned = held[source, :, tile * BLK : (tile + 1) * BLK].T
            first = tile * BLK
            while first < (tile + 1) * BLK:
                part, row = divmod(first, WIDTH)
                size = min((tile + 1) * BLK - first, WIDTH - row)
                skip = first - tile * BLK
                out_ref[part, place * WIDTH + row : place * WIDTH + row + size, :] = turned[skip : skip + size, :]
                first += size


def split_heads(*groups):
    arrays = [pltpu.with_memory_space_constraint(array, pltpu.HBM) for group in groups for array in group]
    counts = tuple(len(group) for group in groups)
    return pl.pallas_call(
        functools.partial(split_kernel, counts),
        out_shape=[jax.ShapeDtypeStruct((PER, WIDTH * count, BLK), BF16) for count in counts],
        in_specs=[HBM] * len(arrays),
        out_specs=[VMEM] * len(counts),
        scratch_shapes=[
            pltpu.VMEM((len(arrays), BLK, PER * WIDTH), BF16),
            pltpu.SemaphoreType.DMA((len(arrays),)),
        ],
        compiler_params=pltpu.CompilerParams(vmem_limit_bytes=49152 * 1024),
        cost_estimate=cost(500_000_000 * len(arrays)),
        name="split_heads",
    )(*arrays)


def join_kernel(in_ref, out_ref):
    out_ref[...] = in_ref[...].reshape(PER * WIDTH, BLK).T


def join_heads(parts):
    return pl.pallas_call(
        join_kernel,
        out_shape=jax.ShapeDtypeStruct((BLK, PER * WIDTH), BF16),
        in_specs=[VMEM],
        out_specs=VMEM,
        compiler_params=LIMIT,
        name="join_heads",
    )(parts)


def both_heads(query):
    row = lax.broadcasted_iota(jnp.int32, (WIDTH, BLK), 0)
    none = jnp.zeros_like(query)
    return jnp.concatenate((jnp.where(row < HDIM, query, none), jnp.where(row < HDIM, none, query)), axis=1)


def diagonal(total):
    return jnp.concatenate((total[:HDIM, :BLK], total[HDIM:, BLK:]), axis=0)


def per_row(stat):
    return jnp.concatenate(
        (
            jnp.broadcast_to(stat[:, :BLK], (HDIM, BLK)),
            jnp.broadcast_to(stat[:, BLK:], (HDIM, BLK)),
        ),
        axis=0,
    )


def fold_rows(values, how):
    return how(values.reshape(BLK // 8, 8, 2 * BLK), axis=0)


def own_kernel(image_ref, kv_ref, q_ref, out_ref, acc_ref, max_ref, den_ref, *scratch):
    bounds, keys, scores, tops, shifts, dens = scratch
    group = lax.axis_index("sup") * PER
    pairs = jnp.int32(0)
    for block in range(PER):
        image = image_ref[group + block]
        first = sum((image_ref[group + j] < image).astype(jnp.int32) for j in range(PER))
        last = sum((image_ref[group + j] <= image).astype(jnp.int32) for j in range(PER))
        bounds[0, block] = first
        bounds[1, block] = last
        pairs += last - first
        keys[block] = kv_ref[block, :WIDTH, :].T
    steps = (pairs + STEP - 1) // STEP
    tops[...] = jnp.full_like(tops, -FAR)
    dens[...] = jnp.zeros_like(dens)
    acc_ref[...] = jnp.zeros_like(acc_ref)

    def advance(at):
        i, j = at
        wrap = j + 1 == bounds[1, i]
        i = jnp.where(wrap, jnp.minimum(i + 1, PER - 1), i)
        return i, jnp.where(wrap, bounds[0, i], j + 1)

    def look(step, at):
        for lane in range(STEP):
            i, j = at
            at = advance(at)
            found = jnp.dot(keys[j], both_heads(q_ref[i]), preferred_element_type=F32)
            scores[step * STEP + lane] = found
            tops[i] = jnp.maximum(tops[i], fold_rows(found, jnp.max))
        return at

    start = (jnp.int32(0), jnp.int32(0))
    lax.fori_loop(0, steps, look, start)
    for block in range(PER):
        top = jnp.max(tops[block], axis=0, keepdims=True)
        max_ref[block] = top
        shifts[block] = top * SCALE_LOG2

    def weigh(step, at):
        for lane in range(STEP):
            pair = step * STEP + lane
            i, j = at
            at = advance(at)
            shift = jnp.where(pair < pairs, shifts[i], FAR)
            weights = jnp.exp2(scores[pair] * SCALE_LOG2 - shift)
            dens[i] += fold_rows(weights, jnp.sum)
            acc_ref[i] += diagonal(jnp.dot(kv_ref[j, WIDTH:, :], weights.astype(BF16), preferred_element_type=F32))
        return at

    lax.fori_loop(0, steps, weigh, start)
    for block in range(PER):
        den = jnp.sum(dens[block], axis=0, keepdims=True)
        den_ref[block] = den
        out_ref[block] = (acc_ref[block] * per_row(1.0 / den)).astype(BF16)


def own_part(image, kv, q):
    return pl.pallas_call(
        own_kernel,
        out_shape=(
            jax.ShapeDtypeStruct((PER, WIDTH, BLK), BF16),
            jax.ShapeDtypeStruct((PER, WIDTH, BLK), F32),
            jax.ShapeDtypeStruct((PER, 1, 2 * BLK), F32),
            jax.ShapeDtypeStruct((PER, 1, 2 * BLK), F32),
        ),
        in_specs=[SMEM, VMEM, VMEM],
        out_specs=(VMEM,) * 4,
        scratch_shapes=[
            pltpu.SMEM((2, PER), jnp.int32),
            pltpu.VMEM((PER, BLK, WIDTH), BF16),
            pltpu.VMEM((PER * PER, BLK, 2 * BLK), F32),
            pltpu.VMEM((PER, 8, 2 * BLK), F32),
            pltpu.VMEM((PER, 1, 2 * BLK), F32),
            pltpu.VMEM((PER, 8, 2 * BLK), F32),
        ],
        compiler_params=LIMIT,
        cost_estimate=cost(100_000_000_000),
        name="own_part",
    )(image, kv, q)


def halo_kernel(turn, image_ref, kv_ref, q_ref, start_ref, acc_ref, max_ref, den_ref, out_ref, *scratch):
    keys, scores, tops, shifts, sums, dens = scratch
    place, places = lax.axis_index("sup"), lax.axis_size("sup")
    from_below = lax.axis_index("core") == turn
    group = place * PER
    image = image_ref[jnp.where(from_below, group, group + PER - 1)]
    beyond = jnp.where(
        from_below, jnp.maximum(group - (PER - 1), 0), jnp.minimum(group + PER, (places - 1) * PER)
    )
    there = jnp.where(from_below, place > 0, place < places - 1)
    count = sum((there & (image_ref[beyond + j] == image)).astype(jnp.int32) for j in range(PER - 1))
    queries = sum((image_ref[group + j] == image).astype(jnp.int32) for j in range(PER))
    pairs = jnp.where(is_late(), 0, count * queries)
    first_query = jnp.where(from_below, 0, PER - queries)
    first_key = jnp.where(from_below, PER - 1 - count, 0)
    steps = (pairs + STEP - 1) // STEP

    def advance(at):
        i, j = at
        wrap = j + 1 == count
        return jnp.where(wrap, jnp.minimum(i + 1, PER - 1), i), jnp.where(wrap, 0, j + 1)

    out_ref[...] = start_ref[...]

    @pl.when(pairs > 0)
    def _():
        for block in range(PER - 1):
            keys[block] = kv_ref[block, :WIDTH, :].T
        for block in range(PER):
            tops[block] = jnp.broadcast_to(max_ref[block], (8, 2 * BLK))

        def look(step, at):
            for lane in range(STEP):
                pair = step * STEP + lane
                i, j = at[0], first_key + at[1]
                at = advance(at)
                found = jnp.dot(keys[j], both_heads(q_ref[i]), preferred_element_type=F32)
                scores[pair] = found
                tops[i] = jnp.maximum(tops[i], fold_rows(found, jnp.max))
            return at

        start = (first_query, jnp.int32(0))
        lax.fori_loop(0, steps, look, start)
        for block in range(PER):
            shifts[block] = jnp.max(tops[block], axis=0, keepdims=True) * SCALE_LOG2
        sums[...] = jnp.zeros_like(sums)
        dens[...] = jnp.zeros_like(dens)

        def weigh(step, at):
            for lane in range(STEP):
                pair = step * STEP + lane
                i, j = at[0], first_key + at[1]
                at = advance(at)
                shift = jnp.where(pair < pairs, shifts[i], FAR)
                weights = jnp.exp2(scores[pair] * SCALE_LOG2 - shift)
                dens[i] += fold_rows(weights, jnp.sum)
                sums[i] += diagonal(jnp.dot(kv_ref[j, WIDTH:, :], weights.astype(BF16), preferred_element_type=F32))
            return at

        lax.fori_loop(0, steps, weigh, start)

        def close(i, carry):
            fade = jnp.exp2(max_ref[i] * SCALE_LOG2 - shifts[i])
            share = 1.0 / (den_ref[i] * fade + jnp.sum(dens[i], axis=0, keepdims=True))
            out_ref[i] = (acc_ref[i] * per_row(fade * share) + sums[i] * per_row(share)).astype(BF16)
            return carry

        lax.fori_loop(first_query, first_query + queries, close, 0)


def halo_part(turn, image, kv, q, start, acc, top, den):
    return pl.pallas_call(
        functools.partial(halo_kernel, turn),
        out_shape=jax.ShapeDtypeStruct((PER, WIDTH, BLK), BF16),
        in_specs=[SMEM] + [VMEM] * 6,
        out_specs=VMEM,
        scratch_shapes=[
            pltpu.VMEM((PER - 1, BLK, WIDTH), BF16),
            pltpu.VMEM((SLOTS, BLK, 2 * BLK), F32),
            pltpu.VMEM((PER, 8, 2 * BLK), F32),
            pltpu.VMEM((PER, 1, 2 * BLK), F32),
            pltpu.VMEM((PER, WIDTH, BLK), F32),
            pltpu.VMEM((PER, 8, 2 * BLK), F32),
        ],
        compiler_params=LIMIT,
        cost_estimate=cost(1_000_000_000),
        name="halo_part",
    )(image, kv, q, start, acc, top, den)


def all_kernel(image_ref, kv_ref, near_ref, far_ref, q_ref, out_ref, *scratch):
    bounds, keys, values, scores, tops, shifts, dens, sums = scratch
    place, places = lax.axis_index("sup"), lax.axis_size("sup")
    group = place * PER
    side = PER - 1

    def held(first, ref):
        for block in range(ref.shape[0]):
            keys[first + block] = ref[block, :WIDTH, :].T
            values[first + block] = ref[block, WIDTH:, :]

    held(side, kv_ref)

    @pl.when(lax.axis_index("core") == 0)
    def _():
        held(0, near_ref)
        held(side + PER, far_ref)

    @pl.when(lax.axis_index("core") != 0)
    def _():
        held(0, far_ref)
        held(side + PER, near_ref)

    lowest, highest = image_ref[group], image_ref[group + PER - 1]
    below, above = jnp.maximum(group - side, 0), jnp.minimum(group + PER, (places - 1) * PER)
    more_below = sum(((place > 0) & (image_ref[below + j] == lowest)).astype(jnp.int32) for j in range(side))
    more_above = sum(
        ((place < places - 1) & (image_ref[above + j] == highest)).astype(jnp.int32) for j in range(side)
    )
    pairs = jnp.int32(0)
    for block in range(PER):
        image = image_ref[group + block]
        first = side + sum((image_ref[group + j] < image).astype(jnp.int32) for j in range(PER))
        last = side + sum((image_ref[group + j] <= image).astype(jnp.int32) for j in range(PER))
        first -= jnp.where(image == lowest, more_below, 0)
        last += jnp.where(image == highest, more_above, 0)
        bounds[0, block] = first
        bounds[1, block] = last
        pairs += last - first
    steps = (pairs + STEP - 1) // STEP
    tops[...] = jnp.full_like(tops, -FAR)
    dens[...] = jnp.zeros_like(dens)
    sums[...] = jnp.zeros_like(sums)

    def advance(at):
        i, j = at
        wrap = j + 1 == bounds[1, i]
        i = jnp.where(wrap, jnp.minimum(i + 1, PER - 1), i)
        return i, jnp.where(wrap, bounds[0, i], j + 1)

    def look(step, at):
        for lane in range(STEP):
            i, j = at
            at = advance(at)
            found = jnp.dot(keys[j], both_heads(q_ref[i]), preferred_element_type=F32)
            scores[step * STEP + lane] = found
            tops[i] = jnp.maximum(tops[i], fold_rows(found, jnp.max))
        return at

    start = (jnp.int32(0), bounds[0, 0])
    lax.fori_loop(0, steps, look, start)
    for block in range(PER):
        shifts[block] = jnp.max(tops[block], axis=0, keepdims=True) * SCALE_LOG2

    def weigh(step, at):
        for lane in range(STEP):
            pair = step * STEP + lane
            i, j = at
            at = advance(at)
            shift = jnp.where(pair < pairs, shifts[i], FAR)
            weights = jnp.exp2(scores[pair] * SCALE_LOG2 - shift)
            dens[i] += fold_rows(weights, jnp.sum)
            sums[i] += diagonal(jnp.dot(values[j], weights.astype(BF16), preferred_element_type=F32))
        return at

    lax.fori_loop(0, steps, weigh, start)
    for block in range(PER):
        den = jnp.sum(dens[block], axis=0, keepdims=True)
        out_ref[block] = (sums[block] * per_row(1.0 / den)).astype(BF16)


def last_kernel(image_ref, kv_ref, near_ref, far_ref, q_ref, start_ref, acc_ref, max_ref, den_ref, out_ref, *scratch):
    bounds, keys, values, scores, tops, shifts, dens, sums = scratch
    late = is_late()

    @pl.when(late)
    def _():
        all_kernel(image_ref, kv_ref, near_ref, far_ref, q_ref, out_ref, *scratch)

    @pl.when(jnp.logical_not(late))
    def _():
        rest = (keys, scores, tops, shifts, sums, dens)
        halo_kernel(1, image_ref, far_ref, q_ref, start_ref, acc_ref, max_ref, den_ref, out_ref, *rest)


def last_part(image, kv, near, far, q, start, acc, top, den):
    blocks = 3 * PER - 2
    return pl.pallas_call(
        last_kernel,
        out_shape=jax.ShapeDtypeStruct((PER, WIDTH, BLK), BF16),
        in_specs=[SMEM] + [VMEM] * 8,
        out_specs=VMEM,
        scratch_shapes=[
            pltpu.SMEM((2, PER), jnp.int32),
            pltpu.VMEM((blocks, BLK, WIDTH), BF16),
            pltpu.VMEM((blocks, WIDTH, BLK), BF16),
            pltpu.VMEM((PER * PER, BLK, 2 * BLK), F32),
            pltpu.VMEM((PER, 8, 2 * BLK), F32),
            pltpu.VMEM((PER, 1, 2 * BLK), F32),
            pltpu.VMEM((PER, 8, 2 * BLK), F32),
            pltpu.VMEM((PER, WIDTH, BLK), F32),
        ],
        compiler_params=LIMIT,
        cost_estimate=cost(1_000_000_000),
        name="last_part",
    )(image, kv, near, far, q, start, acc, top, den)


def pick_kernel(turn, kv_ref, out_ref):
    first = (lax.axis_index("core") == turn).astype(jnp.int32)
    out_ref[...] = kv_ref[pl.ds(first, PER - 1)]


def picked(kv, turn):
    return pl.pallas_call(
        functools.partial(pick_kernel, turn),
        out_shape=jax.ShapeDtypeStruct((PER - 1, 2 * WIDTH, BLK), BF16),
        in_specs=[VMEM],
        out_specs=VMEM,
        compiler_params=LIMIT,
        cost_estimate=cost(1_000_000),
        name="picked",
    )(kv)


def exchanged(kv, turn):
    groups, cores = lax.axis_size("sup"), lax.axis_size("core")
    pairs = []
    for core in range(cores):
        step = 1 if core == turn else -1
        pairs += [
            (group * cores + core, (group + step) * cores + core)
            for group in range(groups)
            if 0 <= group + step < groups
        ]
    part = picked(kv, turn)
    return part, lax.ppermute(part, ("sup", "core"), pairs)


def regrouped(parts):
    return lax.all_to_all(parts, ("core", "grp"), 0, 0, tiled=True)


def body(query_rows, key_rows, value_rows, block_image):
    late = is_late()

    def together(query_rows, key_rows, value_rows):
        (slabs,) = split_heads((query_rows, key_rows, value_rows))
        qkv = regrouped(slabs)
        return qkv[:, WIDTH:], qkv[:, :WIDTH]

    def keys_first(query_rows, key_rows, value_rows):
        slabs, q = split_heads((key_rows, value_rows), (query_rows,))
        return regrouped(slabs), q

    kv, q = lax.cond(late, keys_first, together, query_rows, key_rows, value_rows)
    part, near = exchanged(kv, 0)
    again, part = lax.optimization_barrier((kv, part))
    part, far = exchanged(again, 1)
    part, q = lax.optimization_barrier((part, q))

    def own_now(kv, q):
        return q, *own_part(block_image, kv, q)

    def queries_now(kv, q):
        stat = jnp.zeros((PER, 1, 2 * BLK), F32)
        return regrouped(q), jnp.zeros((PER, WIDTH, BLK), BF16), jnp.zeros((PER, WIDTH, BLK), F32), stat, stat

    q, start, acc, top, den = lax.cond(late, queries_now, own_now, kv, q)
    result = halo_part(0, block_image, near, q, start, acc, top, den)
    result = last_part(block_image, kv, near, far, q, result, acc, top, den)
    return join_heads(regrouped(result))


def solution(mesh):
    per_group = mesh.shape["grp"]
    cores = PER // per_group
    devices = mesh.devices.reshape(-1, cores, per_group)
    inner = jax.sharding.Mesh(devices, ("sup", "core", "grp"))
    rows = P(("sup", "core", "grp"), None)
    return jax.shard_map(
        body,
        mesh=inner,
        in_specs=(rows, rows, rows, P()),
        out_specs=rows,
        check_vma=False,
    )
```

```python
import functools
import math

import jax
import jax.numpy as jnp
from jax import lax
from jax.experimental import pallas as pl
from jax.experimental.pallas import tpu as pltpu
from jax.sharding import PartitionSpec as P

HDIM = 80
BLK = 128
PER = 8
HEADS_HERE = 2
WIDTH = HEADS_HERE * HDIM
TILES = PER * WIDTH // BLK
SCALE_LOG2 = math.log2(math.e) / math.sqrt(HDIM)
FAR = 1e30
SLOTS = 16
STEP = 8
WIDE = 16
RUN = 16
FEW = 4
VMEM = pl.BlockSpec(memory_space=pltpu.VMEM)
SMEM = pl.BlockSpec(memory_space=pltpu.SMEM)
HBM = pl.BlockSpec(memory_space=pltpu.HBM)
LIMIT = pltpu.CompilerParams(vmem_limit_bytes=24 * 1024 * 1024)
F32 = jnp.float32
BF16 = jnp.bfloat16


def cost(flops):
    return pl.CostEstimate(flops=flops, bytes_accessed=1_000_000, transcendentals=0)


def is_late():
    return lax.rem(lax.axis_index("sup"), RUN) >= FEW


def split_kernel(counts, *refs):
    count, outs = sum(counts), len(counts)
    sources, out_refs, (held, sems) = refs[:count], refs[count : count + outs], refs[count + outs :]
    copies = [pltpu.make_async_copy(ref, held.at[place], sems.at[place]) for place, ref in enumerate(sources)]
    for copy in copies:
        copy.start()
    places = [(out_ref, place) for out_ref, many in zip(out_refs, counts) for place in range(many)]
    for source, (out_ref, place) in enumerate(places):
        copies[source].wait()
        for tile in range(TILES):
            turned = held[source, :, tile * BLK : (tile + 1) * BLK].T
            first = tile * BLK
            while first < (tile + 1) * BLK:
                part, row = divmod(first, WIDTH)
                size = min((tile + 1) * BLK - first, WIDTH - row)
                skip = first - tile * BLK
                out_ref[part, place * WIDTH + row : place * WIDTH + row + size, :] = turned[skip : skip + size, :]
                first += size


def split_heads(*groups):
    arrays = [pltpu.with_memory_space_constraint(array, pltpu.HBM) for group in groups for array in group]
    counts = tuple(len(group) for group in groups)
    return pl.pallas_call(
        functools.partial(split_kernel, counts),
        out_shape=[jax.ShapeDtypeStruct((PER, WIDTH * count, BLK), BF16) for count in counts],
        in_specs=[HBM] * len(arrays),
        out_specs=[VMEM] * len(counts),
        scratch_shapes=[
            pltpu.VMEM((len(arrays), BLK, PER * WIDTH), BF16),
            pltpu.SemaphoreType.DMA((len(arrays),)),
        ],
        compiler_params=pltpu.CompilerParams(vmem_limit_bytes=49152 * 1024),
        cost_estimate=cost(500_000_000 * len(arrays)),
        name="split_heads",
    )(*arrays)


def join_kernel(in_ref, out_ref):
    out_ref[...] = in_ref[...].reshape(PER * WIDTH, BLK).T


def join_heads(parts):
    return pl.pallas_call(
        join_kernel,
        out_shape=jax.ShapeDtypeStruct((BLK, PER * WIDTH), BF16),
        in_specs=[VMEM],
        out_specs=VMEM,
        compiler_params=LIMIT,
        name="join_heads",
    )(parts)


def both_heads(query):
    row = lax.broadcasted_iota(jnp.int32, (WIDTH, BLK), 0)
    none = jnp.zeros_like(query)
    return jnp.concatenate((jnp.where(row < HDIM, query, none), jnp.where(row < HDIM, none, query)), axis=1)


def diagonal(total):
    return jnp.concatenate((total[:HDIM, :BLK], total[HDIM:, BLK:]), axis=0)


def per_row(stat):
    return jnp.concatenate(
        (
            jnp.broadcast_to(stat[:, :BLK], (HDIM, BLK)),
            jnp.broadcast_to(stat[:, BLK:], (HDIM, BLK)),
        ),
        axis=0,
    )


def fold_rows(values, how):
    return how(values.reshape(BLK // 8, 8, 2 * BLK), axis=0)


def own_kernel(image_ref, kv_ref, q_ref, out_ref, acc_ref, max_ref, den_ref, *scratch):
    bounds, keys, scores, tops, shifts, dens = scratch
    group = lax.axis_index("sup") * PER
    pairs = jnp.int32(0)
    for block in range(PER):
        image = image_ref[group + block]
        first = sum((image_ref[group + j] < image).astype(jnp.int32) for j in range(PER))
        last = sum((image_ref[group + j] <= image).astype(jnp.int32) for j in range(PER))
        bounds[0, block] = first
        bounds[1, block] = last
        pairs += last - first
        keys[block] = kv_ref[block, :WIDTH, :].T
    steps = (pairs + STEP - 1) // STEP
    tops[...] = jnp.full_like(tops, -FAR)
    dens[...] = jnp.zeros_like(dens)
    acc_ref[...] = jnp.zeros_like(acc_ref)

    def advance(at):
        i, j = at
        wrap = j + 1 == bounds[1, i]
        i = jnp.where(wrap, jnp.minimum(i + 1, PER - 1), i)
        return i, jnp.where(wrap, bounds[0, i], j + 1)

    def look(step, at):
        for lane in range(STEP):
            i, j = at
            at = advance(at)
            found = jnp.dot(keys[j], both_heads(q_ref[i]), preferred_element_type=F32)
            scores[step * STEP + lane] = found
            tops[i] = jnp.maximum(tops[i], fold_rows(found, jnp.max))
        return at

    start = (jnp.int32(0), jnp.int32(0))
    lax.fori_loop(0, steps, look, start)
    for block in range(PER):
        top = jnp.max(tops[block], axis=0, keepdims=True)
        max_ref[block] = top
        shifts[block] = top * SCALE_LOG2

    def weigh(step, at):
        for lane in range(STEP):
            pair = step * STEP + lane
            i, j = at
            at = advance(at)
            shift = jnp.where(pair < pairs, shifts[i], FAR)
            weights = jnp.exp2(scores[pair] * SCALE_LOG2 - shift)
            dens[i] += fold_rows(weights, jnp.sum)
            acc_ref[i] += diagonal(jnp.dot(kv_ref[j, WIDTH:, :], weights.astype(BF16), preferred_element_type=F32))
        return at

    lax.fori_loop(0, steps, weigh, start)
    for block in range(PER):
        den = jnp.sum(dens[block], axis=0, keepdims=True)
        den_ref[block] = den
        out_ref[block] = (acc_ref[block] * per_row(1.0 / den)).astype(BF16)


def own_part(image, kv, q):
    return pl.pallas_call(
        own_kernel,
        out_shape=(
            jax.ShapeDtypeStruct((PER, WIDTH, BLK), BF16),
            jax.ShapeDtypeStruct((PER, WIDTH, BLK), F32),
            jax.ShapeDtypeStruct((PER, 1, 2 * BLK), F32),
            jax.ShapeDtypeStruct((PER, 1, 2 * BLK), F32),
        ),
        in_specs=[SMEM, VMEM, VMEM],
        out_specs=(VMEM,) * 4,
        scratch_shapes=[
            pltpu.SMEM((2, PER), jnp.int32),
            pltpu.VMEM((PER, BLK, WIDTH), BF16),
            pltpu.VMEM((PER * PER, BLK, 2 * BLK), F32),
            pltpu.VMEM((PER, 8, 2 * BLK), F32),
            pltpu.VMEM((PER, 1, 2 * BLK), F32),
            pltpu.VMEM((PER, 8, 2 * BLK), F32),
        ],
        compiler_params=LIMIT,
        cost_estimate=cost(100_000_000_000),
        name="own_part",
    )(image, kv, q)


def halo_kernel(turn, image_ref, kv_ref, q_ref, start_ref, acc_ref, max_ref, den_ref, out_ref, *scratch):
    keys, scores, tops, shifts, sums, dens = scratch
    place, places = lax.axis_index("sup"), lax.axis_size("sup")
    from_below = lax.axis_index("core") == turn
    group = place * PER
    image = image_ref[jnp.where(from_below, group, group + PER - 1)]
    beyond = jnp.where(
        from_below, jnp.maximum(group - (PER - 1), 0), jnp.minimum(group + PER, (places - 1) * PER)
    )
    there = jnp.where(from_below, place > 0, place < places - 1)
    count = sum((there & (image_ref[beyond + j] == image)).astype(jnp.int32) for j in range(PER - 1))
    queries = sum((image_ref[group + j] == image).astype(jnp.int32) for j in range(PER))
    pairs = jnp.where(is_late(), 0, count * queries)
    first_query = jnp.where(from_below, 0, PER - queries)
    first_key = jnp.where(from_below, PER - 1 - count, 0)

    def advance(at):
        i, j = at
        wrap = j + 1 == count
        return jnp.where(wrap, jnp.minimum(i + 1, PER - 1), i), jnp.where(wrap, 0, j + 1)

    out_ref[...] = start_ref[...]

    @pl.when(pairs > 0)
    def _():
        for block in range(PER - 1):
            keys[block] = kv_ref[block, :WIDTH, :].T
        for block in range(PER):
            tops[block] = jnp.broadcast_to(max_ref[block], (8, 2 * BLK))

        def look(lanes, at):
            for pair in range(lanes):
                i, j = at[0], first_key + at[1]
                at = advance(at)
                found = jnp.dot(keys[j], both_heads(q_ref[i]), preferred_element_type=F32)
                scores[pair] = found
                tops[i] = jnp.maximum(tops[i], fold_rows(found, jnp.max))
            return at

        start = (first_query, jnp.int32(0))

        @pl.when(pairs <= STEP)
        def _():
            look(STEP, start)

        @pl.when(pairs > STEP)
        def _():
            look(SLOTS, start)

        for block in range(PER):
            shifts[block] = jnp.max(tops[block], axis=0, keepdims=True) * SCALE_LOG2
        sums[...] = jnp.zeros_like(sums)
        dens[...] = jnp.zeros_like(dens)

        def weigh(lanes, at):
            for pair in range(lanes):
                i, j = at[0], first_key + at[1]
                at = advance(at)
                shift = jnp.where(pair < pairs, shifts[i], FAR)
                weights = jnp.exp2(scores[pair] * SCALE_LOG2 - shift)
                dens[i] += fold_rows(weights, jnp.sum)
                sums[i] += diagonal(jnp.dot(kv_ref[j, WIDTH:, :], weights.astype(BF16), preferred_element_type=F32))
            return at


        @pl.when(pairs <= STEP)
        def _():
            weigh(STEP, start)

        @pl.when(pairs > STEP)
        def _():
            weigh(SLOTS, start)


        def close(i, carry):
            fade = jnp.exp2(max_ref[i] * SCALE_LOG2 - shifts[i])
            share = 1.0 / (den_ref[i] * fade + jnp.sum(dens[i], axis=0, keepdims=True))
            out_ref[i] = (acc_ref[i] * per_row(fade * share) + sums[i] * per_row(share)).astype(BF16)
            return carry

        lax.fori_loop(first_query, first_query + queries, close, 0)


def halo_part(turn, image, kv, q, start, acc, top, den):
    return pl.pallas_call(
        functools.partial(halo_kernel, turn),
        out_shape=jax.ShapeDtypeStruct((PER, WIDTH, BLK), BF16),
        in_specs=[SMEM] + [VMEM] * 6,
        out_specs=VMEM,
        scratch_shapes=[
            pltpu.VMEM((PER - 1, BLK, WIDTH), BF16),
            pltpu.VMEM((SLOTS, BLK, 2 * BLK), F32),
            pltpu.VMEM((PER, 8, 2 * BLK), F32),
            pltpu.VMEM((PER, 1, 2 * BLK), F32),
            pltpu.VMEM((PER, WIDTH, BLK), F32),
            pltpu.VMEM((PER, 8, 2 * BLK), F32),
        ],
        compiler_params=LIMIT,
        cost_estimate=cost(1_000_000_000),
        name="halo_part",
    )(image, kv, q, start, acc, top, den)


def all_kernel(image_ref, kv_ref, near_ref, far_ref, q_ref, out_ref, *scratch):
    bounds, keys, values, scores, tops, shifts, dens, sums = scratch
    place, places = lax.axis_index("sup"), lax.axis_size("sup")
    group = place * PER
    side = PER - 1

    def held(first, ref):
        for block in range(ref.shape[0]):
            keys[first + block] = ref[block, :WIDTH, :].T
            values[first + block] = ref[block, WIDTH:, :]

    held(side, kv_ref)

    @pl.when(lax.axis_index("core") == 0)
    def _():
        held(0, near_ref)
        held(side + PER, far_ref)

    @pl.when(lax.axis_index("core") != 0)
    def _():
        held(0, far_ref)
        held(side + PER, near_ref)

    lowest, highest = image_ref[group], image_ref[group + PER - 1]
    below, above = jnp.maximum(group - side, 0), jnp.minimum(group + PER, (places - 1) * PER)
    more_below = sum(((place > 0) & (image_ref[below + j] == lowest)).astype(jnp.int32) for j in range(side))
    more_above = sum(
        ((place < places - 1) & (image_ref[above + j] == highest)).astype(jnp.int32) for j in range(side)
    )
    pairs = jnp.int32(0)
    for block in range(PER):
        image = image_ref[group + block]
        first = side + sum((image_ref[group + j] < image).astype(jnp.int32) for j in range(PER))
        last = side + sum((image_ref[group + j] <= image).astype(jnp.int32) for j in range(PER))
        first -= jnp.where(image == lowest, more_below, 0)
        last += jnp.where(image == highest, more_above, 0)
        bounds[0, block] = first
        bounds[1, block] = last
        pairs += last - first
    steps = (pairs + WIDE - 1) // WIDE
    tops[...] = jnp.full_like(tops, -FAR)
    dens[...] = jnp.zeros_like(dens)
    sums[...] = jnp.zeros_like(sums)

    def advance(at):
        i, j = at
        wrap = j + 1 == bounds[1, i]
        i = jnp.where(wrap, jnp.minimum(i + 1, PER - 1), i)
        return i, jnp.where(wrap, bounds[0, i], j + 1)

    def look(step, at):
        for lane in range(WIDE):
            i, j = at
            at = advance(at)
            found = jnp.dot(keys[j], both_heads(q_ref[i]), preferred_element_type=F32)
            scores[step * WIDE + lane] = found
            tops[i] = jnp.maximum(tops[i], fold_rows(found, jnp.max))
        return at

    start = (jnp.int32(0), bounds[0, 0])
    lax.fori_loop(0, steps, look, start)
    for block in range(PER):
        shifts[block] = jnp.max(tops[block], axis=0, keepdims=True) * SCALE_LOG2

    def weigh(step, at):
        for lane in range(WIDE):
            pair = step * WIDE + lane
            i, j = at
            at = advance(at)
            shift = jnp.where(pair < pairs, shifts[i], FAR)
            weights = jnp.exp2(scores[pair] * SCALE_LOG2 - shift)
            dens[i] += fold_rows(weights, jnp.sum)
            sums[i] += diagonal(jnp.dot(values[j], weights.astype(BF16), preferred_element_type=F32))
        return at

    lax.fori_loop(0, steps, weigh, start)
    for block in range(PER):
        den = jnp.sum(dens[block], axis=0, keepdims=True)
        out_ref[block] = (sums[block] * per_row(1.0 / den)).astype(BF16)


def last_kernel(image_ref, kv_ref, near_ref, far_ref, q_ref, start_ref, acc_ref, max_ref, den_ref, out_ref, *scratch):
    bounds, keys, values, scores, tops, shifts, dens, sums = scratch
    late = is_late()

    @pl.when(late)
    def _():
        all_kernel(image_ref, kv_ref, near_ref, far_ref, q_ref, out_ref, *scratch)

    @pl.when(jnp.logical_not(late))
    def _():
        rest = (keys, scores, tops, shifts, sums, dens)
        halo_kernel(1, image_ref, far_ref, q_ref, start_ref, acc_ref, max_ref, den_ref, out_ref, *rest)


def last_part(image, kv, near, far, q, start, acc, top, den):
    blocks = 3 * PER - 2
    return pl.pallas_call(
        last_kernel,
        out_shape=jax.ShapeDtypeStruct((PER, WIDTH, BLK), BF16),
        in_specs=[SMEM] + [VMEM] * 8,
        out_specs=VMEM,
        scratch_shapes=[
            pltpu.SMEM((2, PER), jnp.int32),
            pltpu.VMEM((blocks, BLK, WIDTH), BF16),
            pltpu.VMEM((blocks, WIDTH, BLK), BF16),
            pltpu.VMEM((PER * PER, BLK, 2 * BLK), F32),
            pltpu.VMEM((PER, 8, 2 * BLK), F32),
            pltpu.VMEM((PER, 1, 2 * BLK), F32),
            pltpu.VMEM((PER, 8, 2 * BLK), F32),
            pltpu.VMEM((PER, WIDTH, BLK), F32),
        ],
        compiler_params=LIMIT,
        cost_estimate=cost(1_000_000_000),
        name="last_part",
    )(image, kv, near, far, q, start, acc, top, den)


def pick_kernel(turn, kv_ref, out_ref):
    first = (lax.axis_index("core") == turn).astype(jnp.int32)
    out_ref[...] = kv_ref[pl.ds(first, PER - 1)]


def picked(kv, turn):
    return pl.pallas_call(
        functools.partial(pick_kernel, turn),
        out_shape=jax.ShapeDtypeStruct((PER - 1, 2 * WIDTH, BLK), BF16),
        in_specs=[VMEM],
        out_specs=VMEM,
        compiler_params=LIMIT,
        cost_estimate=cost(1_000_000),
        name="picked",
    )(kv)


def exchanged(kv, turn):
    groups, cores = lax.axis_size("sup"), lax.axis_size("core")
    pairs = []
    for core in range(cores):
        step = 1 if core == turn else -1
        pairs += [
            (group * cores + core, (group + step) * cores + core)
            for group in range(groups)
            if 0 <= group + step < groups
        ]
    part = picked(kv, turn)
    return part, lax.ppermute(part, ("sup", "core"), pairs)


def regrouped(parts):
    return lax.all_to_all(parts, ("core", "grp"), 0, 0, tiled=True)


def body(query_rows, key_rows, value_rows, block_image):
    late = is_late()

    def together(query_rows, key_rows, value_rows):
        (slabs,) = split_heads((query_rows, key_rows, value_rows))
        qkv = regrouped(slabs)
        return qkv[:, WIDTH:], qkv[:, :WIDTH]

    def keys_first(query_rows, key_rows, value_rows):
        slabs, q = split_heads((key_rows, value_rows), (query_rows,))
        return regrouped(slabs), q

    kv, q = lax.cond(late, keys_first, together, query_rows, key_rows, value_rows)
    part, near = exchanged(kv, 0)
    again, part = lax.optimization_barrier((kv, part))
    part, far = exchanged(again, 1)
    part, q = lax.optimization_barrier((part, q))

    def own_now(kv, q):
        return q, *own_part(block_image, kv, q)

    def queries_now(kv, q):
        stat = jnp.zeros((PER, 1, 2 * BLK), F32)
        return regrouped(q), jnp.zeros((PER, WIDTH, BLK), BF16), jnp.zeros((PER, WIDTH, BLK), F32), stat, stat

    q, start, acc, top, den = lax.cond(late, queries_now, own_now, kv, q)
    result = halo_part(0, block_image, near, q, start, acc, top, den)
    result = last_part(block_image, kv, near, far, q, result, acc, top, den)
    return join_heads(regrouped(result))


def solution(mesh):
    per_group = mesh.shape["grp"]
    cores = PER // per_group
    devices = mesh.devices.reshape(-1, cores, per_group)
    inner = jax.sharding.Mesh(devices, ("sup", "core", "grp"))
    rows = P(("sup", "core", "grp"), None)
    return jax.shard_map(
        body,
        mesh=inner,
        in_specs=(rows, rows, rows, P()),
        out_specs=rows,
        check_vma=False,
    )
```
